512 devices in a mesh: dp: 32 (over x, z_hi, core), tensor: 16 (over z_lo, y).
Axes of the slice: x: 4, y: 4, z: 16 (z_hi: 4, z_lo: 4; z = z_hi * 4 + z_lo), core: 2. Of those that a mesh axis runs over, the one named last changes fastest.
Arguments:
- activations: bfloat16 [2, 32768, 4096], P(None, 'dp', 'tensor'), may hold values from -6 to 6
- out_grads: bfloat16 [2, 32768, 4096], P(None, 'dp', 'tensor'), may hold values from -6 to 6
- proj_in: bfloat16 [2, 64, 4096], P(None, None, 'tensor'), may hold values from -0.09375 to 0.09375
- proj_out: bfloat16 [2, 64, 4096], P(None, None, 'tensor'), may hold values from -0.09375 to 0.09375
- example_ids: int32 [32, 1024], P('dp'), may hold values from 0 to 15, never falling along the last dimension, each value on 1 to 128 neighbouring positions
- loss_mask: int32 [32, 1024], P('dp'), may hold values 0 or 1
- query_grads: bfloat16 [69632, 2, 4096], P(('dp', 'tensor')), may hold values from -0.009765625 to 0.009765625
Outputs:
- scores: float32 [69632, 512], P(('dp', 'tensor'))
The draws below stay inside these ranges and needn't reach their ends.
Inputs may be any that keep to these rules, and one draw needn't show every extreme that they name: `example_ids`: along each row ids never fall; each of the 16 examples of a row has 1 to 128 tokens, and one has exactly 128.
All inputs are finite; a program needn't handle non-finite values. No bound on the sum of `loss_mask` on one device may be relied on, other than what follows from the above.
Results may differ from the reference program's by a relative error of at most 0.005.
Values may be sent and summed in bfloat16 or wider, within the bound.
A program may use at most 64 MiB of HBM per device.

```python
import math
import jax
import jax.numpy as jnp
import numpy as np
from jax import lax

D = 4096
RANK = 64
LAYERS = 2
MAX_LEN = 128
TOK_DEV = 1024
E_DEV = 16
TOKENS = 32768
EXAMPLES = 512
QUERIES = 69632
N_DP = 32


def plant(values, key, smallest, largest):
    dims = values.shape
    spot = [jax.random.randint(jax.random.fold_in(key, axis), (), 0, dims[axis]) for axis in range(len(dims))]
    values = values.at[tuple(spot)].set(smallest)
    longest = dims.index(max(dims))
    spot[longest] = (spot[longest] + 1) % dims[longest]
    return values.at[tuple(spot)].set(largest)


def level_of(own_key, shape, cuts, low, largest):
    gain = 1.0
    for dim, blocks in cuts:
        steps = jax.random.uniform(jax.random.fold_in(jax.random.fold_in(own_key, 6), dim), (blocks,), jnp.float32, low / len(cuts), largest / len(cuts))
        gain = gain * jnp.repeat(jnp.exp(steps), shape[dim] // blocks).reshape((-1,) + (1,) * (len(shape) - 1 - dim))
    return gain


def length_profile(count, total, limit, skew):
    weights = [(1 << 20) // math.isqrt(standing ** skew) + 1 for standing in range(2, count + 1)]
    spare, holding = total - limit - (count - 1), [1] * (count - 1)
    while spare > 0:
        free = [i for i in range(count - 1) if holding[i] < limit]
        mass, budget = sum([weights[i] for i in free]), spare
        for i in free:
            more = min(limit - holding[i], max(1, budget * weights[i] // mass), spare)
            holding[i] = holding[i] + more
            spare = spare - more
    return np.array([limit] + holding)


def uneven(stream_key, number_of, total, most, slope):
    if number_of == 2:
        one = jax.random.randint(stream_key, (), max(1, total - most), min(most, total - 1) + 1)
        return jnp.stack([one, total - one])
    lengths = jnp.asarray(length_profile(number_of, total, most, slope), jnp.int32)
    pairs = (number_of - 1) // 2
    donor, receiver = lengths[1:1 + 2 * pairs:2], lengths[2:2 + 2 * pairs:2]
    room = jnp.minimum(donor - 1, most - receiver)
    moved = jax.random.randint(jax.random.fold_in(stream_key, 1), (pairs,), 0, 1 << 20) % (room + 1)
    lengths = lengths.at[1:1 + 2 * pairs:2].set(donor - moved).at[2:2 + 2 * pairs:2].set(receiver + moved)
    return lengths[jax.random.permutation(jax.random.fold_in(stream_key, 2), number_of)]


def noise(own_key, shape, scale, bound, split=(), kind=jnp.bfloat16):
    array = jax.random.normal(own_key, shape, jnp.float32) * scale
    if len(split) > 0:
        array = level_of(own_key, shape, split, -0.22, 0.18) * array
    return jnp.clip(array, min=-bound, max=bound).astype(kind)


def setup_inputs(seed: int = 0) -> dict:
    streams_of = jax.random.split(jax.random.key(seed), 8)
    return {
        "activations": noise(streams_of[0], (LAYERS, TOKENS, D), 1.0, 6.0, ((1, 32), (2, 16))),
        "out_grads": noise(streams_of[1], (LAYERS, TOKENS, D), 1.0, 6.0, ((1, 32), (2, 16))),
        "proj_in": noise(streams_of[2], (LAYERS, RANK, D), D ** -0.5, 0.09375, ((2, 16),)),
        "proj_out": noise(streams_of[3], (LAYERS, RANK, D), D ** -0.5, 0.09375, ((2, 16),)),
        "example_ids": jax.vmap(lambda own: jnp.searchsorted(jnp.cumsum(uneven(own, E_DEV, TOK_DEV, MAX_LEN, 1)), jnp.arange(TOK_DEV), side="right"))(jax.random.split(streams_of[4], N_DP)).reshape((N_DP, TOK_DEV)).astype(jnp.int32),
        "loss_mask": plant((jax.random.randint(streams_of[5], (N_DP, TOK_DEV), 0, 4) < 3).astype(jnp.int32), jax.random.fold_in(streams_of[5], 1), 0, 1),
        "query_grads": noise(streams_of[6], (QUERIES, LAYERS, RANK * RANK), 0.0016, 0.009765625, ((0, 512),)),
    }


def form_blocks(grad_low, act_low, local_ids):
    onehot = (local_ids[:, None] == jnp.arange(E_DEV, dtype=jnp.int32)[None, :]).astype(jnp.float32)
    spread = onehot[None, :, :, None] * grad_low.astype(jnp.float32)[:, :, None, :]
    spread = spread.reshape(LAYERS, TOK_DEV, E_DEV * RANK)
    summed = jnp.einsum('ltj,ltk->ljk', act_low.astype(jnp.float32), spread, precision=lax.Precision.HIGHEST)
    summed = summed.reshape(LAYERS, RANK, E_DEV, RANK)
    return jnp.transpose(summed, (2, 0, 3, 1)).reshape(E_DEV, LAYERS * RANK * RANK)


def reference(activations, out_grads, proj_in, proj_out, example_ids, loss_mask, query_grads):
    token_mask = loss_mask.reshape(TOKENS).astype(jnp.float32)
    act_layers = []
    grad_layers = []
    for layer_index in range(LAYERS):
        act_proj = jnp.dot(activations[layer_index], proj_in[layer_index].T, preferred_element_type=jnp.float32)
        grad_proj = jnp.dot(out_grads[layer_index], proj_out[layer_index].T, preferred_element_type=jnp.float32)
        grad_proj = grad_proj * token_mask[:, None]
        act_layers.append(act_proj.astype(jnp.bfloat16))
        grad_layers.append(grad_proj.astype(jnp.bfloat16))
    act_rows = jnp.stack(act_layers).reshape(LAYERS, N_DP, TOK_DEV, RANK).transpose(1, 0, 2, 3)
    grad_rows = jnp.stack(grad_layers).reshape(LAYERS, N_DP, TOK_DEV, RANK).transpose(1, 0, 2, 3)
    blocks = lax.map(lambda row_group: form_blocks(row_group[0], row_group[1], row_group[2]),
                     (grad_rows, act_rows, example_ids))
    blocks = blocks.astype(jnp.bfloat16).reshape(EXAMPLES, LAYERS * RANK * RANK)
    queries = query_grads.reshape(QUERIES, LAYERS * RANK * RANK)
    return jnp.dot(queries, blocks.T, preferred_element_type=jnp.float32)
```

```python
import functools

import jax
import jax.numpy as jnp
from jax import lax
from jax.experimental import pallas as pl
from jax.experimental.pallas import tpu as pltpu
from jax.sharding import PartitionSpec as P

MESH = pl.DeviceIdType.MESH
F32, BF16 = jnp.float32, jnp.bfloat16
NT = (((1,), (1,)), ((), ()))
QROWS = 144


def wrap(v, n):
    return lax.rem(v + 4 * n, n)


def body(
    act, outg, proj_in, proj_out, ids, mask, queries, out,
    part1, recv1, sum1, recv2, act_low, grad_low, ids2, spread, perm, q_raw, q_perm, blocks, part, other,
    q_sem, own_sem, id_sem, s1_send, s1_recv, s2_send, s2_recv, s3_send, s3_recv, z_send, z_recv,
    line_send, line_recv, corner_send, corner_recv, o_send, o_recv,
):
    dp, tensor = lax.axis_index("dp"), lax.axis_index("tensor")
    x, zh, core = dp // 8, dp // 2 % 4, dp % 2
    zl, y = tensor // 4, tensor % 4
    twin = 1 - core
    z = zh * 4 + zl

    def device(dx=0, dy=0, dzh=0, dzl=0, c=core):
        return (
            (wrap(x + dx, 4) * 4 + wrap(zh + dzh, 4)) * 2 + c,
            wrap(zl + dzl, 4) * 4 + wrap(y + dy, 4),
        )

    def remote(src, dst, send, recv, dev):
        return pltpu.make_async_remote_copy(
            src_ref=src, dst_ref=dst, send_sem=send, recv_sem=recv, device_id=dev, device_id_type=MESH
        )

    barrier = pltpu.get_barrier_semaphore()
    peers = [device(dzh=a, dzl=b) for a in range(4) for b in range(4) if (a, b) != (0, 0)]
    peers += [device(dy=d, c=c) for d in (1, 2, 3) for c in (core, twin)]
    peers += [device(dx=d) for d in (1, 2, 3)] + [device(c=twin)]
    for peer in peers:
        pl.semaphore_signal(barrier, inc=1, device_id=peer, device_id_type=MESH)

    own_queries = pltpu.make_async_copy(queries.at[core], q_raw.at[core], own_sem)
    own_queries.start()

    masked = mask[...].astype(F32)
    for layer in range(2):
        a = lax.dot_general(proj_in[layer], act[layer], NT, preferred_element_type=F32)
        g = lax.dot_general(proj_out[layer], outg[layer], NT, preferred_element_type=F32) * masked
        for q in range(4):
            part1[layer, q, 0:16, :] = a[16 * q:16 * q + 16]
            for i in range(4):
                part1[layer, q, 16:32, 256 * i:256 * i + 256] = g[16 * i:16 * i + 16, 256 * q:256 * q + 256]

    pl.semaphore_wait(barrier, len(peers))

    copies1 = []
    for d in (2, 1, 3, 0):
        for other_core in (0, 1):
            if d or other_core:
                k = 2 * d + other_core
                c = twin if other_core else core
                copies1.append(remote(
                    part1.at[c, wrap(y + d, 4)], recv1.at[k], s1_send.at[k], s1_recv.at[k], device(dy=d, c=c)
                ))
    for copy in copies1:
        copy.start()
    ids2[core] = ids[...]
    id_copy = remote(ids, ids2.at[core], id_sem.at[0], id_sem.at[1], device(c=twin))
    id_copy.start()
    q_copy = remote(queries.at[twin], q_raw.at[core], q_sem.at[0], q_sem.at[1], device(c=twin))
    q_copy.start()

    rows = lax.broadcasted_iota(jnp.int32, (1024, 1024), 0)
    cols = lax.broadcasted_iota(jnp.int32, (1024, 1024), 1)
    place = rows // 16 % 4 * 256 + rows // 64 * 16 + rows % 16
    perm[...] = jnp.where(cols == place, 1.0, 0.0).astype(BF16)
    own_queries.wait()
    q_copy.wait()

    def reorder(step, carry):
        r, b = step // 4, lax.rem(step, 4)
        columns = pl.ds(pl.multiple_of(b * 1024, 1024), 1024)
        moved = jnp.dot(q_raw[r, :, columns], perm[...], preferred_element_type=F32).astype(BF16)
        for q in range(4):
            q_perm[q * 4 + b, r] = moved[:, 256 * q:256 * q + 256]
        return carry

    lax.fori_loop(0, 8, reorder, 0)

    for copy in copies1:
        copy.wait()
    for other_core in (0, 1):
        first = recv1[1] if other_core else part1[core, y]
        total = first + recv1[2 + other_core] + recv1[4 + other_core] + recv1[6 + other_core]
        row = twin if other_core else core
        for q in range(4):
            sum1[q, row] = total[:, 256 * q:256 * q + 256]

    copies2 = [
        remote(sum1.at[wrap(zl + d, 4)], recv2.at[d - 1], s2_send.at[d - 1], s2_recv.at[d - 1], device(dzl=d))
        for d in (2, 3, 1)
    ]
    for copy in copies2:
        copy.start()
    for copy in copies2:
        copy.wait()
    low = (sum1[zl] + recv2[0] + recv2[1] + recv2[2]).astype(BF16)
    act_low[zl] = low[:, 0:16]
    grad_low[y] = low[:, 16:32]
    copies3 = []
    for d in (1, 2, 3):
        copies3.append(remote(
            act_low.at[zl], act_low.at[zl], s3_send.at[0, d - 1], s3_recv.at[0, d - 1], device(dzl=d)
        ))
        copies3.append(remote(
            grad_low.at[y], grad_low.at[y], s3_send.at[1, d - 1], s3_recv.at[1, d - 1], device(dy=d)
        ))
    for copy in copies3:
        copy.start()
    id_copy.wait()
    for copy in copies3:
        copy.wait_send()
    for d in (1, 2, 3):
        remote(
            act_low.at[wrap(zl - d, 4)], act_low.at[wrap(zl - d, 4)],
            s3_send.at[0, d - 1], s3_recv.at[0, d - 1], device(dzl=d),
        ).wait_recv()
        remote(
            grad_low.at[wrap(y - d, 4)], grad_low.at[wrap(y - d, 4)],
            s3_send.at[1, d - 1], s3_recv.at[1, d - 1], device(dy=d),
        ).wait_recv()

    lane = lax.broadcasted_iota(jnp.int32, (16, 256), 1)
    repeat = jnp.where(lane % 16 == lax.broadcasted_iota(jnp.int32, (16, 256), 0), 1.0, 0.0).astype(BF16)
    for row in (0, 1):
        sums = jnp.zeros((256, 16), F32)
        for q in range(4):
            here = ids2[row][:, 256 * q:256 * q + 256]
            onehot = lax.broadcasted_iota(jnp.int32, (16, 256), 0) == here
            grads = grad_low[q, row].astype(F32)
            for i in range(16):
                spread[16 * i:16 * i + 16, :] = jnp.where(onehot, grads[i:i + 1], 0.0).astype(BF16)
            sums = sums + lax.dot_general(spread[...], act_low[q, row], NT, preferred_element_type=F32)
        wide = jnp.dot(sums.astype(BF16), repeat, preferred_element_type=F32)
        block = jnp.zeros((16, 256), F32)
        for i in range(16):
            block = block + jnp.where(lane // 16 == i, wide[16 * i:16 * i + 16], 0.0)
        blocks[y, x, z, 16 * row:16 * row + 16, :] = block.astype(BF16)

    z_copies = {}
    for a in (0, 1, 3, 2):
        for b in range(4):
            if (a, b) != (0, 0):
                g = (4 - a) % 4
                z_copies[g, b] = remote(
                    blocks.at[y, x, z], blocks.at[y, x, z], z_send.at[g, b], z_recv.at[g, b], device(dzh=a, dzl=b)
                )
                z_copies[g, b].start()

    def start_of(g):
        return wrap(zh + g, 4) * 4

    def line_copy(g, axis, d, back=False):
        run = pl.ds(start_of(g), 4)
        k = d - 1
        dev = device(dx=d) if axis == 0 else device(dy=d)
        sx = wrap(x - d, 4) if back and axis == 0 else x
        sy = wrap(y - d, 4) if back and axis == 1 else y
        ref = blocks.at[sy, sx, run]
        return remote(ref, ref, line_send.at[g, axis, k], line_recv.at[g, axis, k], dev)

    def corner_copy(g, axis, dx, dy, back=False):
        half = pl.ds(start_of(g) + 2 * axis, 2)
        sx, sy = wrap(x - dx, 4), wrap(y - dy, 4)
        if not back:
            sx, sy = (sx, y) if axis == 0 else (x, sy)
        ref = blocks.at[sy, sx, half]
        dev = device(dy=dy) if axis == 0 else device(dx=dx)
        k = (dx - 1) * 3 + dy - 1
        return remote(ref, ref, corner_send.at[g, axis, k], corner_recv.at[g, axis, k], dev)

    def from_z(g, b):
        ref = blocks.at[y, x, start_of(g) + wrap(zl - b, 4)]
        remote(ref, ref, z_send.at[g, b], z_recv.at[g, b], device(dzl=1)).wait_recv()

    def group_of(step):
        return jnp.where(step < 2, step, 5 - step)

    def score_copy(g):
        zone = wrap(zh + g, 4)
        return remote(part.at[twin, zone], other.at[zone], o_send.at[g], o_recv.at[g], device(c=twin))

    def advance(step, carry):
        @pl.when(step < 4)
        def _():
            g = group_of(step)

            @pl.when(step > 0)
            def _():
                from_z(g, 0)

            for b in (1, 2, 3):
                from_z(g, b)
            for d in (2, 1, 3):
                line_copy(g, 0, d).start()
                line_copy(g, 1, d).start()

        @pl.when((step >= 1) & (step < 5))
        def _():
            g = group_of(step - 1)
            for d in (1, 3, 2):
                line_copy(g, 0, d, back=True).wait_recv()
                for dy in (2, 1, 3):
                    corner_copy(g, 0, d, dy).start()
                line_copy(g, 1, d, back=True).wait_recv()
                for dx in (2, 1, 3):
                    corner_copy(g, 1, dx, d).start()

        @pl.when(step >= 2)
        def _():
            g = group_of(step - 2)
            for dx in (1, 2, 3):
                for dy in (1, 2, 3):
                    corner_copy(g, 0, dx, dy, back=True).wait_recv()
                    corner_copy(g, 1, dx, dy, back=True).wait_recv()
            first = start_of(g)
            scores = jnp.zeros((2 * QROWS, 128), F32)
            for yy in range(4):
                for b in range(4):
                    lhs = q_perm[yy * 4 + b].reshape(2 * QROWS, 256)
                    rhs = blocks[yy, :, first + b].reshape(128, 256)
                    scores = scores + lax.dot_general(lhs, rhs, NT, preferred_element_type=F32)
            zone = wrap(zh + g, 4)
            part[0, zone] = scores[:QROWS]
            part[1, zone] = scores[QROWS:]
            score_copy(g).start()

        return carry

    lax.fori_loop(0, 6, advance, 0)

    def finish(step, carry):
        for axis in (0, 1):
            for d in (1, 2, 3):
                line_copy(step, axis, d).wait_send()
                for e in (1, 2, 3):
                    corner_copy(step, axis, d, e).wait_send()
        zone = wrap(zh + step, 4)
        ref = other.at[zone]
        remote(part.at[twin, zone], ref, o_send.at[step], o_recv.at[step], device(c=twin)).wait()
        return carry

    lax.fori_loop(0, 4, finish, 0)
    for copy in z_copies.values():
        copy.wait_send()

    sums = [part[core, g] + other[g] for g in range(4)]
    for xx in range(4):
        pieces = [sums[g][:136, 32 * xx:32 * xx + 32] for g in range(4)]
        out[:, 128 * xx:128 * xx + 128] = jnp.concatenate(pieces, axis=1)


def local(activations, out_grads, proj_in, proj_out, example_ids, loss_mask, query_grads):
    queries = jnp.pad(jnp.transpose(query_grads, (1, 0, 2)), ((0, 0), (0, QROWS - 136), (0, 0)))
    vmem = pl.BlockSpec(memory_space=pltpu.VMEM)
    dma = pltpu.SemaphoreType.DMA
    return pl.pallas_call(
        body,
        out_shape=jax.ShapeDtypeStruct((136, 512), F32),
        in_specs=[vmem] * 6 + [pl.BlockSpec(memory_space=pl.ANY)],
        out_specs=vmem,
        scratch_shapes=[
            pltpu.VMEM((2, 4, 32, 1024), F32),
            pltpu.VMEM((8, 32, 1024), F32),
            pltpu.VMEM((4, 2, 32, 256), F32),
            pltpu.VMEM((3, 2, 32, 256), F32),
            pltpu.VMEM((4, 2, 16, 256), BF16),
            pltpu.VMEM((4, 2, 16, 256), BF16),
            pltpu.VMEM((2, 1, 1024), jnp.int32),
            pltpu.VMEM((256, 256), BF16),
            pltpu.VMEM((1024, 1024), BF16),
            pltpu.VMEM((2, QROWS, 4096), BF16),
            pltpu.VMEM((16, 2, QROWS, 256), BF16),
            pltpu.VMEM((4, 4, 16, 32, 256), BF16),
            pltpu.VMEM((2, 4, QROWS, 128), F32),
            pltpu.VMEM((4, QROWS, 128), F32),
            dma((2,)), dma, dma((2,)), dma((8,)), dma((8,)), dma((3,)), dma((3,)), dma((2, 3)), dma((2, 3)),
            dma((4, 4)), dma((4, 4)), dma((4, 2, 3)), dma((4, 2, 3)), dma((4, 2, 9)), dma((4, 2, 9)),
            dma((4,)), dma((4,)),
        ],
        compiler_params=pltpu.CompilerParams(
            collective_id=0, has_side_effects=True, vmem_limit_bytes=48 * 2**20
        ),
        name="scores",
    )(activations, out_grads, proj_in, proj_out, example_ids, loss_mask, queries)


def solution(mesh):
    in_specs = (
        P(None, "dp", "tensor"),
        P(None, "dp", "tensor"),
        P(None, None, "tensor"),
        P(None, None, "tensor"),
        P("dp", None),
        P("dp", None),
        P(("dp", "tensor"), None, None),
    )
    out_specs = P(("dp", "tensor"), None)
    return jax.shard_map(local, mesh=mesh, in_specs=in_specs, out_specs=out_specs, check_vma=False)
```

```python
import jax
import jax.numpy as jnp
from jax import lax
from jax.experimental import pallas as pl
from jax.experimental.pallas import tpu as pltpu
from jax.sharding import PartitionSpec as P

MESH = pl.DeviceIdType.MESH
F32, BF16 = jnp.float32, jnp.bfloat16
NT = (((1,), (1,)), ((), ()))
QROWS = 144


def wrap(v, n):
    return lax.rem(v + 4 * n, n)


def body(
    act_hbm, outg_hbm, in_hbm, out_hbm, ids_hbm, mask_hbm, queries, out,
    act, outg, proj_in, proj_out, ids, mask, q_pairs, q_wide, q_twin,
    part1, relay, mixed, recv1, sum1, recv2, act_low, grad_low, ids2, spread, perm, q_raw, q_perm, blocks, part, other,
    vouch, in_sem, q_sem, id_sem, r_send, r_recv, s1_send, s1_recv, s2_send, s2_recv, s3_send, s3_recv, z_send, z_recv,
    xy_send, xy_recv, o_send, o_recv,
):
    dp, tensor = lax.axis_index("dp"), lax.axis_index("tensor")
    x, zh, core = dp // 8, dp // 2 % 4, dp % 2
    zl, y = tensor // 4, tensor % 4
    twin = 1 - core
    z = zh * 4 + zl

    def device(dx=0, dy=0, dzh=0, dzl=0, c=core):
        return (
            (wrap(x + dx, 4) * 4 + wrap(zh + dzh, 4)) * 2 + c,
            wrap(zl + dzl, 4) * 4 + wrap(y + dy, 4),
        )

    def remote(src, dst, send, recv, dev):
        return pltpu.make_async_remote_copy(
            src_ref=src, dst_ref=dst, send_sem=send, recv_sem=recv, device_id=dev, device_id_type=MESH
        )

    def along(d):
        to = lax.rem(z + 16 + d, 16)
        return ((x * 4 + to // 4) * 2 + core, lax.rem(to, 4) * 4 + y)

    barrier = pltpu.get_barrier_semaphore()
    peers = [along(d) for d in (4, -4, 3, -3, 2, -2, 1, -1)]
    peers += [device(dy=d, c=c) for d in (1, 3) for c in (core, twin)]
    peers += [device(dy=2), device(dx=1), device(dx=2), device(dx=3), device(c=twin)]
    for peer in peers:
        pl.semaphore_signal(barrier, inc=1, device_id=peer, device_id_type=MESH)

    loads = [
        pltpu.make_async_copy(src, dst, in_sem.at[k])
        for k, (src, dst) in enumerate([
            (in_hbm, proj_in), (act_hbm, act), (out_hbm, proj_out), (mask_hbm, mask), (outg_hbm, outg),
            (ids_hbm, ids), (queries, q_pairs),
        ])
    ]
    for load in loads:
        load.start()

    loads[0].wait()
    loads[1].wait()

    def project_act(layer, carry):
        a = lax.dot_general(proj_in[layer], act[layer], NT, preferred_element_type=F32)
        for q in range(4):
            part1[q, layer, 0] = a[16 * q:16 * q + 16]
        return carry

    lax.fori_loop(0, 2, project_act, 0)
    for load in loads[2:5]:
        load.wait()

    def project_grad(layer, carry):
        g = lax.dot_general(proj_out[layer], outg[layer], NT, preferred_element_type=F32) * mask[...].astype(F32)
        for q in range(4):
            for i in range(4):
                part1[q, layer, 1, :, 256 * i:256 * i + 256] = g[16 * i:16 * i + 16, 256 * q:256 * q + 256]
        return carry

    lax.fori_loop(0, 2, project_grad, 0)

    pl.semaphore_wait(barrier, len(peers))
    pl.semaphore_signal(vouch.at[0], inc=1, device_id=along(4), device_id_type=MESH)
    pl.semaphore_signal(vouch.at[1], inc=1, device_id=along(-4), device_id_type=MESH)

    def relay_copy(half):
        d = 3 if half else 1
        return remote(
            part1.at[wrap(y + 2, 4), :, half], relay.at[half], r_send.at[half], r_recv.at[half], device(dy=d)
        )

    def plain_copy(half, cross):
        d = 1 if half else 3
        c = twin if cross else core
        return remote(
            part1.at[wrap(y + d, 4), c, half], recv1.at[cross, 0, half], s1_send.at[cross, 0, half],
            s1_recv.at[cross, 0, half], device(dy=d, c=c),
        )

    def mixed_copy(half, cross):
        d = 3 if half else 1
        c = twin if cross else core
        return remote(
            mixed.at[half, c], recv1.at[cross, 1, half], s1_send.at[cross, 1, half],
            s1_recv.at[cross, 1, half], device(dy=d, c=c),
        )

    twin_copy = remote(part1.at[y, twin], recv1.at[1, 2], s1_send.at[0, 2, 0], s1_recv.at[0, 2, 0], device(c=twin))
    both = [(half, cross) for cross in (0, 1) for half in (0, 1)]
    for half in (0, 1):
        relay_copy(half).start()
    for half, cross in both:
        plain_copy(half, cross).start()
    twin_copy.start()
    loads[5].wait()
    ids2[core] = ids[...]
    id_copy = remote(ids, ids2.at[core], id_sem.at[0], id_sem.at[1], device(c=twin))
    id_copy.start()

    loads[6].wait()

    def widen(step, carry):
        rows = pl.ds(pl.multiple_of(step * 512, 512), 512)
        q_wide[rows, :] = q_pairs[rows, :].astype(F32)
        return carry

    lax.fori_loop(0, 17, widen, 0)
    filler = jnp.zeros((QROWS - 136, 128), F32)

    def pick(layer, dst):
        def one(step, carry):
            rows = q_wide[pl.ds(2 * step + layer, 136, stride=64), :]
            dst[:, pl.ds(pl.multiple_of(step * 128, 128), 128)] = jnp.concatenate([rows, filler], axis=0).astype(BF16)
            return carry

        lax.fori_loop(0, 32, one, 0)

    pick(twin, q_twin)
    q_copy = remote(q_twin, q_raw.at[core], q_sem.at[0], q_sem.at[1], device(c=twin))
    q_copy.start()

    for half in (0, 1):
        relay_copy(half).wait()
        mixed[half] = relay[half] + part1[wrap(y + (3 if half else 1), 4), :, half]
        for cross in (0, 1):
            mixed_copy(half, cross).start()

    pick(core, q_raw.at[core])
    row = lax.broadcasted_iota(jnp.int32, (512, 1), 0)
    place = lax.rem(row // 16, 4) * 128 + row // 64 * 16 + lax.rem(row, 16)
    perm[...] = jnp.where(lax.broadcasted_iota(jnp.int32, (512, 512), 1) == place, 1.0, 0.0).astype(BF16)

    for half, cross in both:
        plain_copy(half, cross).wait()
        mixed_copy(half, cross).wait()
    twin_copy.wait()
    for cross in (0, 1):
        mine = recv1[1, 2] if cross else part1[y, core]
        total = mine + recv1[cross, 0] + recv1[cross, 1]
        for q in range(4):
            sum1[q, twin if cross else core] = total[:, :, 256 * q:256 * q + 256].reshape(32, 256)

    copies2 = [
        remote(sum1.at[wrap(zl + d, 4)], recv2.at[d - 1], s2_send.at[d - 1], s2_recv.at[d - 1], device(dzl=d))
        for d in (2, 3, 1)
    ]
    for copy in copies2:
        copy.start()
    q_copy.wait()

    def reorder(step, carry):
        b, half = step // 2, lax.rem(step, 2)
        columns = pl.ds(pl.multiple_of(step * 512, 512), 512)
        into = pl.ds(pl.multiple_of(half * 128, 128), 128)
        lhs = q_raw[:, :, columns].reshape(2 * QROWS, 512)
        moved = jnp.dot(lhs, perm[...], preferred_element_type=F32).astype(BF16).reshape(2, QROWS, 512)
        for q in range(4):
            q_perm[q * 4 + b, :, :, into] = moved[:, :, 128 * q:128 * q + 128]
        return carry

    lax.fori_loop(0, 8, reorder, 0)
    for copy in copies2:
        copy.wait()
    low = (sum1[zl] + recv2[0] + recv2[1] + recv2[2]).astype(BF16)
    act_low[zl] = low[:, 0:16]
    grad_low[y] = low[:, 16:32]
    copies3 = []
    for d in (1, 2, 3):
        copies3.append(remote(
            act_low.at[zl], act_low.at[zl], s3_send.at[0, d - 1], s3_recv.at[0, d - 1], device(dzl=d)
        ))
        copies3.append(remote(
            grad_low.at[y], grad_low.at[y], s3_send.at[1, d - 1], s3_recv.at[1, d - 1], device(dy=d)
        ))
    for copy in copies3:
        copy.start()
    id_copy.wait()
    for copy in copies3:
        copy.wait_send()
    for d in (1, 2, 3):
        remote(
            act_low.at[wrap(zl - d, 4)], act_low.at[wrap(zl - d, 4)],
            s3_send.at[0, d - 1], s3_recv.at[0, d - 1], device(dzl=d),
        ).wait_recv()
        remote(
            grad_low.at[wrap(y - d, 4)], grad_low.at[wrap(y - d, 4)],
            s3_send.at[1, d - 1], s3_recv.at[1, d - 1], device(dy=d),
        ).wait_recv()

    lane = lax.broadcasted_iota(jnp.int32, (16, 256), 1)
    repeat = jnp.where(lane % 16 == lax.broadcasted_iota(jnp.int32, (16, 256), 0), 1.0, 0.0).astype(BF16)

    def form(row, carry):
        def add(q, sums):
            here = ids2[row, :, pl.ds(pl.multiple_of(q * 256, 256), 256)]
            onehot = lax.broadcasted_iota(jnp.int32, (16, 256), 0) == here
            grads = grad_low[q, row].astype(F32)
            for i in range(16):
                spread[16 * i:16 * i + 16, :] = jnp.where(onehot, grads[i:i + 1], 0.0).astype(BF16)
            return sums + lax.dot_general(spread[...], act_low[q, row], NT, preferred_element_type=F32)

        sums = lax.fori_loop(0, 4, add, jnp.zeros((256, 16), F32))
        wide = jnp.dot(sums.astype(BF16), repeat, preferred_element_type=F32)
        block = jnp.zeros((16, 256), F32)
        for i in range(16):
            block = block + jnp.where(lane // 16 == i, wide[16 * i:16 * i + 16], 0.0)
        blocks[0, 0, 0, 0, 0, pl.ds(pl.multiple_of(16 * row, 16), 16), :] = block.astype(BF16)
        return carry

    lax.fori_loop(0, 2, form, 0)

    slot_of = (0, 1, 3, 2)

    pl.semaphore_wait(vouch.at[0], 1)
    pl.semaphore_wait(vouch.at[1], 1)
    z_copies = {}
    for a in (0, 1, 3, 2):
        for b in (1, 3, 2, 0):
            if (a, b) != (0, 0):
                slot, k = slot_of[(4 - a) % 4], (4 - b) % 4
                z_copies[slot, k] = remote(
                    blocks.at[0, 0, 0, 0, 0], blocks.at[slot, k // 2, 0, 0, k % 2], z_send.at[slot, k],
                    z_recv.at[slot, k], device(dzh=a, dzl=b),
                )
                z_copies[slot, k].start()

    ways = [device(dx=1), device(dx=3), device(dy=1), device(dy=3), device(dx=2), device(dy=2)]

    def stage(slot, n):
        at = lambda *k: blocks.at[(slot,) + k]
        all_, rest = slice(None), pl.ds(1, 3)
        if slot == 3 and n == 0:
            src = [at(all_, 0, 0)] * 6
            dst = [at(all_, 0, 3), at(all_, 0, 1), at(all_, 3, 0), at(all_, 1, 0), at(all_, 0, 2), at(all_, 2, 0)]
        elif slot == 3:
            src = [at(1, rest, 0)] * 2 + [at(0, 0, rest)] * 2 + [at(1, rest, 0), at(0, 0, rest)]
            dst = [at(1, rest, 3), at(1, rest, 1), at(0, 3, rest), at(0, 1, rest), at(1, rest, 2), at(0, 2, rest)]
        elif n == 0:
            src = [at(all_, 0, 0)] * 4
            dst = [at(all_, 0, 3), at(all_, 0, 1), at(all_, 3, 0), at(all_, 1, 0)]
        elif n == 1:
            src = [at(0, 0, 3), at(1, 0, 1), at(0, 3, 0), at(1, 1, 0)]
            dst = [at(0, 0, 2), at(1, 0, 2), at(0, 2, 0), at(1, 2, 0)]
        elif n == 2:
            src = [at(1, rest, 0)] * 2 + [at(0, 0, rest)] * 2
            dst = [at(1, rest, 3), at(1, rest, 1), at(0, 3, rest), at(0, 1, rest)]
        else:
            src = [at(1, rest, 3, 0), at(1, rest, 1, 1), at(0, 3, rest, 0), at(0, 1, rest, 1)]
            dst = [at(1, rest, 2, 0), at(1, rest, 2, 1), at(0, 2, rest, 0), at(0, 2, rest, 1)]
        return [
            remote(src[k], dst[k], xy_send.at[slot, n, k], xy_recv.at[slot, n, k], ways[k])
            for k in range(len(src))
        ]

    count = (4, 4, 4, 2)
    stages = {(slot, n): stage(slot, n) for slot in range(4) for n in range(count[slot])}
    score_copies = [
        remote(part.at[twin, slot], other.at[slot], o_send.at[slot], o_recv.at[slot], device(c=twin))
        for slot in range(4)
    ]

    def go(slot, n):
        if n == 0:
            for k in range(4):
                if (slot, k) != (0, 0):
                    z_copies[slot, k].wait_recv()
        else:
            for copy in stages[slot, n - 1]:
                copy.wait_recv()
        if n < count[slot]:
            for copy in stages[slot, n]:
                copy.start()

    def score(slot):
        def add(dy, scores):
            for k in range(4):
                lhs = q_perm[wrap(y + dy, 4) * 4 + wrap(zl + k, 4)].reshape(2 * QROWS, 256)
                rhs = blocks[slot, k // 2, dy, :, k % 2].reshape(128, 256)
                scores = scores + lax.dot_general(lhs, rhs, NT, preferred_element_type=F32)
            return scores

        scores = lax.fori_loop(0, 4, add, jnp.zeros((2 * QROWS, 128), F32))
        part[0, slot] = scores[:QROWS]
        part[1, slot] = scores[QROWS:]
        score_copies[slot].start()

    order = [
        (0, 0), (0, 1), (1, 0), (2, 0), (0, 2), (1, 1), (2, 1), (0, 3), (3, 0), (1, 2), (2, 2), (0, 4), (3, 1),
        (1, 3), (2, 3), (1, 4), (2, 4), (3, 2),
    ]
    for slot, n in order:
        go(slot, n)
        if n == count[slot]:
            score(slot)

    for copy in z_copies.values():
        copy.wait_send()
    for copies in stages.values():
        for copy in copies:
            copy.wait_send()
    for copy in score_copies:
        copy.wait()

    sums = [part[core, slot_of[r]] + other[slot_of[r]] for r in range(4)]
    for dx in range(4):
        pieces = [sums[r][:136, 32 * dx:32 * dx + 32] for r in range(4)]
        piece = pltpu.roll(jnp.concatenate(pieces, axis=1), zh * 32, 1)
        out[:, pl.ds(pl.multiple_of(wrap(x + dx, 4) * 128, 128), 128)] = piece


def local(activations, out_grads, proj_in, proj_out, example_ids, loss_mask, query_grads):
    queries = query_grads.reshape(136, 2, 32, 128).transpose(0, 2, 1, 3).reshape(136 * 64, 128)
    dma = pltpu.SemaphoreType.DMA
    return pl.pallas_call(
        body,
        out_shape=jax.ShapeDtypeStruct((136, 512), F32),
        in_specs=[pl.BlockSpec(memory_space=pl.ANY)] * 7,
        out_specs=pl.BlockSpec(memory_space=pltpu.VMEM),
        scratch_shapes=[
            pltpu.VMEM((2, 1024, 256), BF16),
            pltpu.VMEM((2, 1024, 256), BF16),
            pltpu.VMEM((2, 64, 256), BF16),
            pltpu.VMEM((2, 64, 256), BF16),
            pltpu.VMEM((1, 1024), jnp.int32),
            pltpu.VMEM((1, 1024), jnp.int32),
            pltpu.VMEM((136 * 64, 128), BF16),
            pltpu.VMEM((136 * 64, 128), F32),
            pltpu.VMEM((QROWS, 4096), BF16),
            pltpu.VMEM((4, 2, 2, 16, 1024), F32),
            pltpu.VMEM((2, 2, 16, 1024), F32),
            pltpu.VMEM((2, 2, 16, 1024), F32),
            pltpu.VMEM((2, 3, 2, 16, 1024), F32),
            pltpu.VMEM((4, 2, 32, 256), F32),
            pltpu.VMEM((3, 2, 32, 256), F32),
            pltpu.VMEM((4, 2, 16, 256), BF16),
            pltpu.VMEM((4, 2, 16, 256), BF16),
            pltpu.VMEM((2, 1, 1024), jnp.int32),
            pltpu.VMEM((256, 256), BF16),
            pltpu.VMEM((512, 512), BF16),
            pltpu.VMEM((2, QROWS, 4096), BF16),
            pltpu.VMEM((16, 2, QROWS, 256), BF16),
            pltpu.VMEM((4, 2, 4, 4, 2, 32, 256), BF16),
            pltpu.VMEM((2, 4, QROWS, 128), F32),
            pltpu.VMEM((4, QROWS, 128), F32),
            pltpu.SemaphoreType.REGULAR((2,)), dma((7,)), dma((2,)), dma((2,)), dma((2,)), dma((2,)), dma((2, 3, 2)), dma((2, 3, 2)),
            dma((3,)), dma((3,)), dma((2, 3)), dma((2, 3)), dma((4, 4)), dma((4, 4)),
            dma((4, 4, 6)), dma((4, 4, 6)), dma((4,)), dma((4,)),
        ],
        compiler_params=pltpu.CompilerParams(
            collective_id=0, has_side_effects=True, vmem_limit_bytes=56 * 2**20
        ),
        name="scores",
    )(activations, out_grads, proj_in, proj_out, example_ids, loss_mask, queries)


def solution(mesh):
    in_specs = (
        P(None, "dp", "tensor"),
        P(None, "dp", "tensor"),
        P(None, None, "tensor"),
        P(None, None, "tensor"),
        P("dp", None),
        P("dp", None),
        P(("dp", "tensor"), None, None),
    )
    out_specs = P(("dp", "tensor"), None)
    return jax.shard_map(local, mesh=mesh, in_specs=in_specs, out_specs=out_specs, check_vma=False)
```

```python
import jax
import jax.numpy as jnp
from jax import lax
from jax.experimental import pallas as pl
from jax.experimental.pallas import tpu as pltpu
from jax.sharding import PartitionSpec as P

MESH = pl.DeviceIdType.MESH
F32, BF16 = jnp.float32, jnp.bfloat16
NT = (((1,), (1,)), ((), ()))
QROWS = 144


def wrap(v, n):
    return lax.rem(v + 4 * n, n)


def body(
    act_hbm, outg_hbm, in_hbm, out_hbm, ids_hbm, mask_hbm, queries, out,
    act, outg, proj_in, proj_out, ids, mask, q_pairs, q_wide, q_twin,
    part1, relay, mixed, recv1, sum1, recv2, act_low, grad_low, ids2, spread, perm, q_raw, q_perm, blocks, part, other,
    in_sem, q_sem, id_sem, r_send, r_recv, s1_send, s1_recv, s2_send, s2_recv, s3_send, s3_recv, z1_send, z1_recv, z2_send, z2_recv,
    xy_send, xy_recv, o_send, o_recv,
):
    dp, tensor = lax.axis_index("dp"), lax.axis_index("tensor")
    x, zh, core = dp // 8, dp // 2 % 4, dp % 2
    zl, y = tensor // 4, tensor % 4
    twin = 1 - core
    z = zh * 4 + zl

    def device(dx=0, dy=0, dzh=0, dzl=0, c=core):
        return (
            (wrap(x + dx, 4) * 4 + wrap(zh + dzh, 4)) * 2 + c,
            wrap(zl + dzl, 4) * 4 + wrap(y + dy, 4),
        )

    def remote(src, dst, send, recv, dev):
        return pltpu.make_async_remote_copy(
            src_ref=src, dst_ref=dst, send_sem=send, recv_sem=recv, device_id=dev, device_id_type=MESH
        )

    def along(d):
        to = lax.rem(z + 16 + d, 16)
        return ((x * 4 + to // 4) * 2 + core, lax.rem(to, 4) * 4 + y)

    barrier = pltpu.get_barrier_semaphore()
    peers = [along(d) for d in (4, -4, 3, -3, 2, -2, 1, -1)]
    peers += [device(dy=d, c=c) for d in (1, 3) for c in (core, twin)]
    peers += [device(dy=2), device(dx=1), device(dx=3), device(c=twin)]
    for peer in peers:
        pl.semaphore_signal(barrier, inc=1, device_id=peer, device_id_type=MESH)

    loads = [
        pltpu.make_async_copy(src, dst, in_sem.at[k])
        for k, (src, dst) in enumerate([
            (in_hbm, proj_in), (act_hbm, act), (out_hbm, proj_out), (mask_hbm, mask), (outg_hbm, outg),
            (ids_hbm, ids), (queries, q_pairs),
        ])
    ]
    for load in loads:
        load.start()

    loads[0].wait()
    loads[1].wait()

    def project_act(layer, carry):
        a = lax.dot_general(proj_in[layer], act[layer], NT, preferred_element_type=F32)
        for q in range(4):
            part1[q, layer, 0] = a[16 * q:16 * q + 16]
        return carry

    lax.fori_loop(0, 2, project_act, 0)
    pl.semaphore_wait(barrier, len(peers))

    def relay_copy(half):
        d = 3 if half else 1
        return remote(
            part1.at[wrap(y + 2, 4), :, half], relay.at[half], r_send.at[half], r_recv.at[half], device(dy=d)
        )

    def plain_copy(half, cross):
        d = 1 if half else 3
        c = twin if cross else core
        return remote(
            part1.at[wrap(y + d, 4), c, half], recv1.at[cross, 0, half], s1_send.at[cross, 0, half],
            s1_recv.at[cross, 0, half], device(dy=d, c=c),
        )

    def mixed_copy(half, cross):
        d = 3 if half else 1
        c = twin if cross else core
        return remote(
            mixed.at[half, c], recv1.at[cross, 1, half], s1_send.at[cross, 1, half],
            s1_recv.at[cross, 1, half], device(dy=d, c=c),
        )

    def twin_copy(half):
        return remote(
            part1.at[y, twin, half], recv1.at[1, 2, half], s1_send.at[0, 2, half], s1_recv.at[0, 2, half],
            device(c=twin),
        )

    relay_copy(0).start()
    for cross in (0, 1):
        plain_copy(0, cross).start()
    twin_copy(0).start()
    for load in loads[2:5]:
        load.wait()

    def project_grad(layer, carry):
        g = lax.dot_general(proj_out[layer], outg[layer], NT, preferred_element_type=F32) * mask[...].astype(F32)
        for q in range(4):
            for i in range(4):
                part1[q, layer, 1, :, 256 * i:256 * i + 256] = g[16 * i:16 * i + 16, 256 * q:256 * q + 256]
        return carry

    lax.fori_loop(0, 2, project_grad, 0)

    relay_copy(1).start()
    for cross in (0, 1):
        plain_copy(1, cross).start()
    twin_copy(1).start()
    loads[5].wait()
    ids2[core] = ids[...]
    id_copy = remote(ids, ids2.at[core], id_sem.at[0], id_sem.at[1], device(c=twin))
    id_copy.start()

    loads[6].wait()

    def widen(step, carry):
        rows = pl.ds(pl.multiple_of(step * 512, 512), 512)
        q_wide[rows, :] = q_pairs[rows, :].astype(F32)
        return carry

    lax.fori_loop(0, 17, widen, 0)
    filler = jnp.zeros((QROWS - 136, 128), F32)

    def pick(layer, dst):
        def one(step, carry):
            rows = q_wide[pl.ds(2 * step + layer, 136, stride=64), :]
            dst[:, pl.ds(pl.multiple_of(step * 128, 128), 128)] = jnp.concatenate([rows, filler], axis=0).astype(BF16)
            return carry

        lax.fori_loop(0, 32, one, 0)

    pick(twin, q_twin)
    q_copy = remote(q_twin, q_raw.at[core], q_sem.at[0], q_sem.at[1], device(c=twin))
    q_copy.start()

    for half in (0, 1):
        relay_copy(half).wait()
        mixed[half] = relay[half] + part1[wrap(y + (3 if half else 1), 4), :, half]
        for cross in (0, 1):
            mixed_copy(half, cross).start()

    pick(core, q_raw.at[core])
    row = lax.broadcasted_iota(jnp.int32, (512, 1), 0)
    place = lax.rem(row // 16, 4) * 128 + row // 64 * 16 + lax.rem(row, 16)
    perm[...] = jnp.where(lax.broadcasted_iota(jnp.int32, (512, 512), 1) == place, 1.0, 0.0).astype(BF16)

    def second_copies(half):
        return [
            remote(
                sum1.at[half, wrap(zl + d, 4)], recv2.at[half, d - 1], s2_send.at[half, d - 1],
                s2_recv.at[half, d - 1], device(dzl=d),
            )
            for d in (2, 3, 1)
        ]

    for half in (0, 1):
        for cross in (0, 1):
            plain_copy(half, cross).wait()
            mixed_copy(half, cross).wait()
        twin_copy(half).wait()
        for cross in (0, 1):
            mine = recv1[1, 2, half] if cross else part1[y, core, half]
            total = mine + recv1[cross, 0, half] + recv1[cross, 1, half]
            for q in range(4):
                sum1[half, q, twin if cross else core] = total[:, 256 * q:256 * q + 256]
        for copy in second_copies(half):
            copy.start()

    def third_copies(half):
        low, place = (grad_low, y) if half else (act_low, zl)
        return [
            remote(
                low.at[place], low.at[place], s3_send.at[half, d - 1], s3_recv.at[half, d - 1],
                device(dy=d) if half else device(dzl=d),
            )
            for d in (2, 1, 3)
        ]

    for half in (0, 1):
        for copy in second_copies(half):
            copy.wait()
        total = (sum1[half, zl] + recv2[half, 0] + recv2[half, 1] + recv2[half, 2]).astype(BF16)
        if half:
            grad_low[y] = total
        else:
            act_low[zl] = total
        for copy in third_copies(half):
            copy.start()

    q_copy.wait()

    def reorder(step, carry):
        b, half = step // 2, lax.rem(step, 2)
        columns = pl.ds(pl.multiple_of(step * 512, 512), 512)
        into = pl.ds(pl.multiple_of(half * 128, 128), 128)
        lhs = q_raw[:, :, columns].reshape(2 * QROWS, 512)
        moved = jnp.dot(lhs, perm[...], preferred_element_type=F32).astype(BF16).reshape(2, QROWS, 512)
        for q in range(4):
            q_perm[q * 4 + b, :, :, into] = moved[:, :, 128 * q:128 * q + 128]
        return carry

    lax.fori_loop(0, 8, reorder, 0)
    id_copy.wait()
    for half in (0, 1):
        for copy in third_copies(half):
            copy.wait_send()
    for d in (1, 2, 3):
        remote(
            act_low.at[wrap(zl - d, 4)], act_low.at[wrap(zl - d, 4)],
            s3_send.at[0, d - 1], s3_recv.at[0, d - 1], device(dzl=d),
        ).wait_recv()
        remote(
            grad_low.at[wrap(y - d, 4)], grad_low.at[wrap(y - d, 4)],
            s3_send.at[1, d - 1], s3_recv.at[1, d - 1], device(dy=d),
        ).wait_recv()

    lane = lax.broadcasted_iota(jnp.int32, (16, 256), 1)
    repeat = jnp.where(lane % 16 == lax.broadcasted_iota(jnp.int32, (16, 256), 0), 1.0, 0.0).astype(BF16)

    for row in (0, 1):
        sums = jnp.zeros((256, 16), F32)
        for q in range(4):
            onehot = lax.broadcasted_iota(jnp.int32, (16, 256), 0) == ids2[row, :, 256 * q:256 * q + 256]
            grads = grad_low[q, row].astype(F32)
            for i in range(16):
                spread[16 * i:16 * i + 16, :] = jnp.where(onehot, grads[i:i + 1], 0.0).astype(BF16)
            sums = sums + lax.dot_general(spread[...], act_low[q, row], NT, preferred_element_type=F32)
        wide = jnp.dot(sums.astype(BF16), repeat, preferred_element_type=F32)
        block = jnp.zeros((16, 256), F32)
        for i in range(16):
            block = block + jnp.where(lane // 16 == i, wide[16 * i:16 * i + 16], 0.0)
        blocks[row, 0, 0, 4] = block.astype(BF16)

    reach = (1, 2, 3, 4, -1, -2, -3, -4)
    z1 = {
        d: remote(
            blocks.at[:, 0, 0, 4], blocks.at[:, 0, 0, 4 - d], z1_send.at[k], z1_recv.at[k], along(d)
        )
        for k, d in enumerate(reach)
    }
    for d in (-1, -2, -3, -4, 1, 2, 3, 4):
        z1[d].start()
    beyond = [
        remote(
            blocks.at[:, 0, 0, pl.ds(5, 4)], blocks.at[:, 0, 0, pl.ds(9, 4)], z2_send.at[0], z2_recv.at[0], along(-4)
        ),
        remote(
            blocks.at[:, 0, 0, pl.ds(1, 3)], blocks.at[:, 0, 0, pl.ds(13, 3)], z2_send.at[1], z2_recv.at[1], along(4)
        ),
    ]
    ways = [device(dx=1), device(dx=3), device(dy=1), device(dy=3)]
    groups = (((3, 2), (5, 1)), ((6, 1), (7, 2)), ((0, 2), (2, 1)), ((9, 2), (11, 2)), ((13, 1), (14, 2)))

    def stage(group, n):
        (start, one), (middle, two) = groups[group]
        whole, lower, upper = pl.ds(start, one + two), pl.ds(start, one), pl.ds(middle, two)
        at, both, rest = (lambda *k: blocks.at[k]), slice(None), pl.ds(1, 3)
        if n == 0:
            src = [at(both, 0, 0, whole)] * 4
            dst = [at(both, 0, 3, whole), at(both, 0, 1, whole), at(both, 3, 0, whole), at(both, 1, 0, whole)]
        elif n == 1:
            src = [at(0, 0, 3, whole), at(1, 0, 1, whole), at(0, 3, 0, whole), at(1, 1, 0, whole)]
            dst = [at(0, 0, 2, whole), at(1, 0, 2, whole), at(0, 2, 0, whole), at(1, 2, 0, whole)]
        elif n == 2:
            src = [at(1, rest, 0, whole)] * 2 + [at(0, 0, rest, whole)] * 2
            dst = [at(1, rest, 3, whole), at(1, rest, 1, whole), at(0, 3, rest, whole), at(0, 1, rest, whole)]
        else:
            src = [at(1, rest, 3, lower), at(1, rest, 1, upper), at(0, 3, rest, lower), at(0, 1, rest, upper)]
            dst = [at(1, rest, 2, lower), at(1, rest, 2, upper), at(0, 2, rest, lower), at(0, 2, rest, upper)]
        return [
            remote(src[k], dst[k], xy_send.at[group, n, k], xy_recv.at[group, n, k], ways[k]) for k in range(4)
        ]

    stages = {(group, n): stage(group, n) for group in range(5) for n in range(4)}

    def go(group, n):
        if n:
            before = stages[group, n - 1]
        else:
            before = ([z1[1], z1[-1]], [z1[-2], z1[-3], z1[-4]], [z1[2], z1[3], z1[4]], beyond[:1], beyond[1:])[group]
        for copy in before:
            copy.wait_recv()
        if n < 4:
            for copy in stages[group, n]:
                copy.start()

    def score(group):
        (start, one), (_, two) = groups[group]

        def one_place(place, carry):
            far = lax.rem(z + place + 12, 16)
            zone, b = far // 4, lax.rem(far, 4)
            scores = jnp.zeros((2 * QROWS, 128), F32)
            for dy in range(4):
                lhs = q_perm[wrap(y + dy, 4) * 4 + b].reshape(2 * QROWS, 256)
                rhs = jnp.concatenate(
                    [blocks[half, dy, dx, place] for dx in range(4) for half in (0, 1)], axis=0
                )
                scores = scores + lax.dot_general(lhs, rhs, NT, preferred_element_type=F32)
            part[0, zone] += scores[:QROWS]
            part[1, zone] += scores[QROWS:]
            return carry

        lax.fori_loop(start, start + one + two, one_place, 0)

    part[...] = jnp.zeros_like(part)
    near, far = (0, 1, 2), (3, 4)
    for groups_now, n in [
        (near, 0), (near, 1), (far, 0), (near, 2), (far, 1), (far, 2), (near, 3), (far, 3), (near, 4), (far, 4)
    ]:
        for group in groups_now:
            go(group, n)
            if n == 4:
                score(group)
            if n == 0 and group in (1, 2):
                beyond[group - 1].start()
    swap = remote(part.at[twin], other, o_send.at[0], o_recv.at[0], device(c=twin))
    swap.start()

    for copy in z1.values():
        copy.wait_send()
    for copy in beyond:
        copy.wait_send()
    for copies in stages.values():
        for copy in copies:
            copy.wait_send()
    swap.wait()

    for dx in range(4):
        cols = slice(32 * dx, 32 * dx + 32)
        pieces = [(part[core, zone] + other[zone])[:136, cols] for zone in range(4)]
        out[:, pl.ds(pl.multiple_of(wrap(x + dx, 4) * 128, 128), 128)] = jnp.concatenate(pieces, axis=1)


def local(activations, out_grads, proj_in, proj_out, example_ids, loss_mask, query_grads):
    queries = query_grads.reshape(136, 2, 32, 128).transpose(0, 2, 1, 3).reshape(136 * 64, 128)
    dma = pltpu.SemaphoreType.DMA
    return pl.pallas_call(
        body,
        out_shape=jax.ShapeDtypeStruct((136, 512), F32),
        in_specs=[pl.BlockSpec(memory_space=pl.ANY)] * 7,
        out_specs=pl.BlockSpec(memory_space=pltpu.VMEM),
        scratch_shapes=[
            pltpu.VMEM((2, 1024, 256), BF16),
            pltpu.VMEM((2, 1024, 256), BF16),
            pltpu.VMEM((2, 64, 256), BF16),
            pltpu.VMEM((2, 64, 256), BF16),
            pltpu.VMEM((1, 1024), jnp.int32),
            pltpu.VMEM((1, 1024), jnp.int32),
            pltpu.VMEM((136 * 64, 128), BF16),
            pltpu.VMEM((136 * 64, 128), F32),
            pltpu.VMEM((QROWS, 4096), BF16),
            pltpu.VMEM((4, 2, 2, 16, 1024), F32),
            pltpu.VMEM((2, 2, 16, 1024), F32),
            pltpu.VMEM((2, 2, 16, 1024), F32),
            pltpu.VMEM((2, 3, 2, 16, 1024), F32),
            pltpu.VMEM((2, 4, 2, 16, 256), F32),
            pltpu.VMEM((2, 3, 2, 16, 256), F32),
            pltpu.VMEM((4, 2, 16, 256), BF16),
            pltpu.VMEM((4, 2, 16, 256), BF16),
            pltpu.VMEM((2, 1, 1024), jnp.int32),
            pltpu.VMEM((256, 256), BF16),
            pltpu.VMEM((512, 512), BF16),
            pltpu.VMEM((2, QROWS, 4096), BF16),
            pltpu.VMEM((16, 2, QROWS, 256), BF16),
            pltpu.VMEM((2, 4, 4, 16, 16, 256), BF16),
            pltpu.VMEM((2, 4, QROWS, 128), F32),
            pltpu.VMEM((4, QROWS, 128), F32),
            dma((7,)), dma((2,)), dma((2,)), dma((2,)), dma((2,)), dma((2, 3, 2)), dma((2, 3, 2)),
            dma((2, 3)), dma((2, 3)), dma((2, 3)), dma((2, 3)), dma((8,)), dma((8,)), dma((2,)), dma((2,)),
            dma((5, 4, 4)), dma((5, 4, 4)), dma((1,)), dma((1,)),
        ],
        compiler_params=pltpu.CompilerParams(
            collective_id=0, has_side_effects=True, vmem_limit_bytes=56 * 2**20
        ),
        name="scores",
    )(activations, out_grads, proj_in, proj_out, example_ids, loss_mask, queries)


def solution(mesh):
    in_specs = (
        P(None, "dp", "tensor"),
        P(None, "dp", "tensor"),
        P(None, None, "tensor"),
        P(None, None, "tensor"),
        P("dp", None),
        P("dp", None),
        P(("dp", "tensor"), None, None),
    )
    out_specs = P(("dp", "tensor"), None)
    return jax.shard_map(local, mesh=mesh, in_specs=in_specs, out_specs=out_specs, check_vma=False)
```

```python
import jax
import jax.numpy as jnp
from jax import lax
from jax.experimental import pallas as pl
from jax.experimental.pallas import tpu as pltpu
from jax.sharding import PartitionSpec as P

MESH = pl.DeviceIdType.MESH
F32, BF16 = jnp.float32, jnp.bfloat16
NT = (((1,), (1,)), ((), ()))
QROWS = 144


def wrap(v, n):
    return lax.rem(v + 4 * n, n)


def body(
    act_hbm, outg_hbm, in_hbm, out_hbm, ids_hbm, mask_hbm, queries, out, got,
    act, outg, proj_in, proj_out, ids, mask, q_pairs, q_wide, q_twin,
    part1, relay, mixed, recv1, sum1, recv2, act_low, grad_low, ids2, spread, perm, q_raw, q_perm, blocks, part, kept, theirs,
    in_sem, q_sem, id_sem, r_send, r_recv, s1_send, s1_recv, s2_send, s2_recv, s3_send, s3_recv, z1_send, z1_recv, z2_send, z2_recv,
    xy_send, xy_recv, o_send, o_recv, keep_sem,
):
    dp, tensor = lax.axis_index("dp"), lax.axis_index("tensor")
    x, zh, core = dp // 8, dp // 2 % 4, dp % 2
    zl, y = tensor // 4, tensor % 4
    twin = 1 - core
    z = zh * 4 + zl

    def device(dx=0, dy=0, dzh=0, dzl=0, c=core):
        return (
            (wrap(x + dx, 4) * 4 + wrap(zh + dzh, 4)) * 2 + c,
            wrap(zl + dzl, 4) * 4 + wrap(y + dy, 4),
        )

    def remote(src, dst, send, recv, dev):
        return pltpu.make_async_remote_copy(
            src_ref=src, dst_ref=dst, send_sem=send, recv_sem=recv, device_id=dev, device_id_type=MESH
        )

    loads = [
        pltpu.make_async_copy(src, dst, in_sem.at[k])
        for k, (src, dst) in enumerate([
            (in_hbm, proj_in), (act_hbm, act), (out_hbm, proj_out), (mask_hbm, mask), (outg_hbm, outg),
            (ids_hbm, ids), (queries, q_pairs),
        ])
    ]
    for load in loads:
        load.start()

    def along(d):
        to = lax.rem(z + 16 + d, 16)
        return ((x * 4 + to // 4) * 2 + core, lax.rem(to, 4) * 4 + y)

    barrier = pltpu.get_barrier_semaphore()
    peers = [along(d) for d in (4, -4, 3, -3, 2, -2, 1, -1)]
    peers += [device(dy=d, c=c) for d in (1, 3) for c in (core, twin)]
    peers += [device(dy=2), device(dx=1), device(dx=3), device(c=twin)]
    for peer in peers:
        pl.semaphore_signal(barrier, inc=1, device_id=peer, device_id_type=MESH)

    loads[0].wait()
    loads[1].wait()

    def project_act(layer, carry):
        a = lax.dot_general(proj_in[layer], act[layer], NT, preferred_element_type=F32)
        for q in range(4):
            part1[q, layer, 0] = a[16 * q:16 * q + 16]
        return carry

    lax.fori_loop(0, 2, project_act, 0)
    pl.semaphore_wait(barrier, len(peers))

    def relay_copy(half):
        d = 3 if half else 1
        return remote(
            part1.at[wrap(y + 2, 4), :, half], relay.at[half], r_send.at[half], r_recv.at[half], device(dy=d)
        )

    def plain_copy(half, cross):
        d = 1 if half else 3
        c = twin if cross else core
        return remote(
            part1.at[wrap(y + d, 4), c, half], recv1.at[cross, 0, half], s1_send.at[cross, 0, half],
            s1_recv.at[cross, 0, half], device(dy=d, c=c),
        )

    def mixed_copy(half, cross):
        d = 3 if half else 1
        c = twin if cross else core
        return remote(
            mixed.at[half, c], recv1.at[cross, 1, half], s1_send.at[cross, 1, half],
            s1_recv.at[cross, 1, half], device(dy=d, c=c),
        )

    def twin_copy(half):
        return remote(
            part1.at[y, twin, half], recv1.at[1, 2, half], s1_send.at[0, 2, half], s1_recv.at[0, 2, half],
            device(c=twin),
        )

    relay_copy(0).start()
    for cross in (0, 1):
        plain_copy(0, cross).start()
    twin_copy(0).start()
    for load in loads[2:5]:
        load.wait()

    def project_grad(layer, carry):
        g = lax.dot_general(proj_out[layer], outg[layer], NT, preferred_element_type=F32) * mask[...].astype(F32)
        for q in range(4):
            for i in range(4):
                part1[q, layer, 1, :, 256 * i:256 * i + 256] = g[16 * i:16 * i + 16, 256 * q:256 * q + 256]
        return carry

    lax.fori_loop(0, 2, project_grad, 0)

    relay_copy(1).start()
    for cross in (0, 1):
        plain_copy(1, cross).start()
    twin_copy(1).start()
    loads[5].wait()
    ids2[core] = ids[...]
    id_copy = remote(ids, ids2.at[core], id_sem.at[0], id_sem.at[1], device(c=twin))
    id_copy.start()

    loads[6].wait()

    def widen(step, carry):
        rows = pl.ds(pl.multiple_of(step * 512, 512), 512)
        q_wide[rows, :] = q_pairs[rows, :].astype(F32)
        return carry

    lax.fori_loop(0, 17, widen, 0)
    filler = jnp.zeros((QROWS - 136, 128), F32)

    def pick(layer, dst):
        def one(step, carry):
            rows = q_wide[pl.ds(2 * step + layer, 136, stride=64), :]
            dst[:, pl.ds(pl.multiple_of(step * 128, 128), 128)] = jnp.concatenate([rows, filler], axis=0).astype(BF16)
            return carry

        lax.fori_loop(0, 32, one, 0)

    pick(twin, q_twin)
    q_copy = remote(q_twin, q_raw.at[core], q_sem.at[0], q_sem.at[1], device(c=twin))
    q_copy.start()

    for half in (0, 1):
        relay_copy(half).wait()
        mixed[half] = relay[half] + part1[wrap(y + (3 if half else 1), 4), :, half]
        for cross in (0, 1):
            mixed_copy(half, cross).start()

    pick(core, q_raw.at[core])
    row = lax.broadcasted_iota(jnp.int32, (512, 1), 0)
    place = lax.rem(row // 16, 4) * 128 + row // 64 * 16 + lax.rem(row, 16)
    perm[...] = jnp.where(lax.broadcasted_iota(jnp.int32, (512, 512), 1) == place, 1.0, 0.0).astype(BF16)

    def second_copies(half):
        return [
            remote(
                sum1.at[half, wrap(zl + d, 4)], recv2.at[half, d - 1], s2_send.at[half, d - 1],
                s2_recv.at[half, d - 1], device(dzl=d),
            )
            for d in (2, 3, 1)
        ]

    for half in (0, 1):
        for cross in (0, 1):
            plain_copy(half, cross).wait()
            mixed_copy(half, cross).wait()
        twin_copy(half).wait()
        for cross in (0, 1):
            mine = recv1[1, 2, half] if cross else part1[y, core, half]
            total = mine + recv1[cross, 0, half] + recv1[cross, 1, half]
            for q in range(4):
                sum1[half, q, twin if cross else core] = total[:, 256 * q:256 * q + 256]
        for copy in second_copies(half):
            copy.start()

    q_copy.wait()

    def reorder(step, carry):
        b, half = step // 2, lax.rem(step, 2)
        columns = pl.ds(pl.multiple_of(step * 512, 512), 512)
        into = pl.ds(pl.multiple_of(half * 128, 128), 128)
        lhs = q_raw[:, :, columns].reshape(2 * QROWS, 512)
        moved = jnp.dot(lhs, perm[...], preferred_element_type=F32).astype(BF16).reshape(2, QROWS, 512)
        for q in range(4):
            q_perm[q * 4 + b, :, :, into] = moved[:, :, 128 * q:128 * q + 128]
        return carry

    lax.fori_loop(0, 4, reorder, 0)

    def third_copies(half):
        low, place = (grad_low, y) if half else (act_low, zl)
        return [
            remote(
                low.at[place], low.at[place], s3_send.at[half, d - 1], s3_recv.at[half, d - 1],
                device(dy=d) if half else device(dzl=d),
            )
            for d in (2, 1, 3)
        ]

    for half in (0, 1):
        for copy in second_copies(half):
            copy.wait()
        total = (sum1[half, zl] + recv2[half, 0] + recv2[half, 1] + recv2[half, 2]).astype(BF16)
        if half:
            grad_low[y] = total
        else:
            act_low[zl] = total
        for copy in third_copies(half):
            copy.start()

    lax.fori_loop(4, 8, reorder, 0)
    id_copy.wait()
    for half in (0, 1):
        for copy in third_copies(half):
            copy.wait_send()
    for d in (1, 2, 3):
        remote(
            act_low.at[wrap(zl - d, 4)], act_low.at[wrap(zl - d, 4)],
            s3_send.at[0, d - 1], s3_recv.at[0, d - 1], device(dzl=d),
        ).wait_recv()
        remote(
            grad_low.at[wrap(y - d, 4)], grad_low.at[wrap(y - d, 4)],
            s3_send.at[1, d - 1], s3_recv.at[1, d - 1], device(dy=d),
        ).wait_recv()

    lane = lax.broadcasted_iota(jnp.int32, (16, 256), 1)
    repeat = jnp.where(lane % 16 == lax.broadcasted_iota(jnp.int32, (16, 256), 0), 1.0, 0.0).astype(BF16)

    for row in (0, 1):
        sums = jnp.zeros((256, 16), F32)
        for q in range(4):
            onehot = lax.broadcasted_iota(jnp.int32, (16, 256), 0) == ids2[row, :, 256 * q:256 * q + 256]
            grads = grad_low[q, row].astype(F32)
            for i in range(16):
                spread[16 * i:16 * i + 16, :] = jnp.where(onehot, grads[i:i + 1], 0.0).astype(BF16)
            sums = sums + lax.dot_general(spread[...], act_low[q, row], NT, preferred_element_type=F32)
        wide = jnp.dot(sums.astype(BF16), repeat, preferred_element_type=F32)
        block = jnp.zeros((16, 256), F32)
        for i in range(16):
            block = block + jnp.where(lane // 16 == i, wide[16 * i:16 * i + 16], 0.0)
        blocks[row, 0, 0, 4] = block.astype(BF16)

    reach = (1, 2, 3, 4, -1, -2, -3, -4)
    z1 = {
        d: remote(
            blocks.at[:, 0, 0, 4], blocks.at[:, 0, 0, 4 - d], z1_send.at[k], z1_recv.at[k], along(d)
        )
        for k, d in enumerate(reach)
    }
    for d in (-1, -2, -3, -4, 1, 2, 3, 4):
        z1[d].start()
    beyond = [
        remote(
            blocks.at[:, 0, 0, pl.ds(5, 4)], blocks.at[:, 0, 0, pl.ds(9, 4)], z2_send.at[0], z2_recv.at[0], along(-4)
        ),
        remote(
            blocks.at[:, 0, 0, pl.ds(1, 3)], blocks.at[:, 0, 0, pl.ds(13, 3)], z2_send.at[1], z2_recv.at[1], along(4)
        ),
    ]
    ways = [device(dx=1), device(dx=3), device(dy=1), device(dy=3)]
    groups = (((3, 2), (5, 1)), ((6, 1), (7, 2)), ((0, 2), (2, 1)), ((9, 2), (11, 2)), ((13, 1), (14, 2)))

    def stage(group, n):
        (start, one), (middle, two) = groups[group]
        whole, lower, upper = pl.ds(start, one + two), pl.ds(start, one), pl.ds(middle, two)
        at, both, rest = (lambda *k: blocks.at[k]), slice(None), pl.ds(1, 3)
        if n == 0:
            src = [at(both, 0, 0, whole)] * 4
            dst = [at(both, 0, 3, whole), at(both, 0, 1, whole), at(both, 3, 0, whole), at(both, 1, 0, whole)]
        elif n == 1:
            src = [at(0, 0, 3, whole), at(1, 0, 1, whole), at(0, 3, 0, whole), at(1, 1, 0, whole)]
            dst = [at(0, 0, 2, whole), at(1, 0, 2, whole), at(0, 2, 0, whole), at(1, 2, 0, whole)]
        elif n == 2:
            src = [at(1, rest, 0, whole)] * 2 + [at(0, 0, rest, whole)] * 2
            dst = [at(1, rest, 3, whole), at(1, rest, 1, whole), at(0, 3, rest, whole), at(0, 1, rest, whole)]
        else:
            src = [at(1, rest, 3, lower), at(1, rest, 1, upper), at(0, 3, rest, lower), at(0, 1, rest, upper)]
            dst = [at(1, rest, 2, lower), at(1, rest, 2, upper), at(0, 2, rest, lower), at(0, 2, rest, upper)]
        return [
            remote(src[k], dst[k], xy_send.at[group, n, k], xy_recv.at[group, n, k], ways[k]) for k in range(4)
        ]

    stages = {(group, n): stage(group, n) for group in range(5) for n in range(4)}

    def go(group, n):
        if n:
            before = stages[group, n - 1]
        else:
            before = ([z1[1], z1[-1]], [z1[-2], z1[-3], z1[-4]], [z1[2], z1[3], z1[4]], beyond[:1], beyond[1:])[group]
        for copy in before:
            copy.wait_recv()
        if n < 4:
            for copy in stages[group, n]:
                copy.start()

    def score(start, pairs, single, who=None):
        def add(place, places):
            far = lax.rem(z + place + 12, 16)
            zone, b = far // 4, lax.rem(far, 4)
            scores = jnp.zeros(((2 if who is None else 1) * QROWS, 128 * len(places)), F32)
            for dy in range(4):
                k = wrap(y + dy, 4) * 4 + b
                lhs = q_perm[k].reshape(2 * QROWS, 256) if who is None else q_perm[k, who]
                rhs = jnp.concatenate(
                    [blocks[half, dy, dx, place + e] for e in places for dx in range(4) for half in (0, 1)], axis=0
                )
                scores = scores + lax.dot_general(lhs, rhs, NT, preferred_element_type=F32)
            for k in range(len(places)):
                for n, rows in enumerate((0, 1) if who is None else (who,)):
                    part[rows, lax.rem(zone + k, 4)] += scores[QROWS * n:QROWS * n + QROWS, 128 * k:128 * k + 128]

        def add_pair(place, carry):
            add(place, (0, 4))
            return carry

        lax.fori_loop(start, start + pairs, add_pair, 0)
        add(single, (0,))

    part[...] = jnp.zeros_like(part)
    near, far = (0, 1, 2), (3, 4)
    for groups_now, n in [
        (near, 0), (near, 1), (far, 0), (far, 1), (near, 2), (far, 2), (near, 3), (far, 3), (near, 4), (far, 4)
    ]:
        for group in groups_now:
            go(group, n)
            if n == 0 and group in (1, 2):
                beyond[group - 1].start()
        if n == 4 and groups_now == near:
            score(0, 4, 8)

    def arrange(rows, into):
        for dx in range(4):
            cols = slice(32 * dx, 32 * dx + 32)
            pieces = [part[rows, zone][:136, cols] for zone in range(4)]
            into[:, pl.ds(pl.multiple_of(wrap(x + dx, 4) * 128, 128), 128)] = jnp.concatenate(pieces, axis=1)

    score(9, 3, 12, twin)
    arrange(twin, theirs)
    swap = remote(theirs, got, o_send.at[0], o_recv.at[0], device(c=twin))
    swap.start()
    score(9, 3, 12, core)
    arrange(core, kept)
    keep = pltpu.make_async_copy(kept, out, keep_sem)
    keep.start()

    for copy in z1.values():
        copy.wait_send()
    for copy in beyond:
        copy.wait_send()
    for copies in stages.values():
        for copy in copies:
            copy.wait_send()
    keep.wait()
    swap.wait()


def local(activations, out_grads, proj_in, proj_out, example_ids, loss_mask, query_grads):
    queries = query_grads.reshape(136, 2, 32, 128).transpose(0, 2, 1, 3).reshape(136 * 64, 128)
    dma = pltpu.SemaphoreType.DMA
    own, received = pl.pallas_call(
        body,
        out_shape=[jax.ShapeDtypeStruct((136, 512), F32)] * 2,
        in_specs=[pl.BlockSpec(memory_space=pl.ANY)] * 7,
        out_specs=[pl.BlockSpec(memory_space=pl.ANY)] * 2,
        scratch_shapes=[
            pltpu.VMEM((2, 1024, 256), BF16),
            pltpu.VMEM((2, 1024, 256), BF16),
            pltpu.VMEM((2, 64, 256), BF16),
            pltpu.VMEM((2, 64, 256), BF16),
            pltpu.VMEM((1, 1024), jnp.int32),
            pltpu.VMEM((1, 1024), jnp.int32),
            pltpu.VMEM((136 * 64, 128), BF16),
            pltpu.VMEM((136 * 64, 128), F32),
            pltpu.VMEM((QROWS, 4096), BF16),
            pltpu.VMEM((4, 2, 2, 16, 1024), F32),
            pltpu.VMEM((2, 2, 16, 1024), F32),
            pltpu.VMEM((2, 2, 16, 1024), F32),
            pltpu.VMEM((2, 3, 2, 16, 1024), F32),
            pltpu.VMEM((2, 4, 2, 16, 256), F32),
            pltpu.VMEM((2, 3, 2, 16, 256), F32),
            pltpu.VMEM((4, 2, 16, 256), BF16),
            pltpu.VMEM((4, 2, 16, 256), BF16),
            pltpu.VMEM((2, 1, 1024), jnp.int32),
            pltpu.VMEM((256, 256), BF16),
            pltpu.VMEM((512, 512), BF16),
            pltpu.VMEM((2, QROWS, 4096), BF16),
            pltpu.VMEM((16, 2, QROWS, 256), BF16),
            pltpu.VMEM((2, 4, 4, 16, 16, 256), BF16),
            pltpu.VMEM((2, 4, QROWS, 128), F32),
            pltpu.VMEM((136, 512), F32),
            pltpu.VMEM((136, 512), F32),
            dma((7,)), dma((2,)), dma((2,)), dma((2,)), dma((2,)), dma((2, 3, 2)), dma((2, 3, 2)),
            dma((2, 3)), dma((2, 3)), dma((2, 3)), dma((2, 3)), dma((8,)), dma((8,)), dma((2,)), dma((2,)),
            dma((5, 4, 4)), dma((5, 4, 4)), dma((1,)), dma((1,)), dma,
        ],
        compiler_params=pltpu.CompilerParams(
            collective_id=0, has_side_effects=True, vmem_limit_bytes=56 * 2**20
        ),
        name="scores",
    )(activations, out_grads, proj_in, proj_out, example_ids, loss_mask, queries)
    return own + received


def solution(mesh):
    in_specs = (
        P(None, "dp", "tensor"),
        P(None, "dp", "tensor"),
        P(None, None, "tensor"),
        P(None, None, "tensor"),
        P("dp", None),
        P("dp", None),
        P(("dp", "tensor"), None, None),
    )
    out_specs = P(("dp", "tensor"), None)
    return jax.shard_map(local, mesh=mesh, in_specs=in_specs, out_specs=out_specs, check_vma=False)
```

```python
import jax
import jax.numpy as jnp
from jax import lax
from jax.experimental import pallas as pl
from jax.experimental.pallas import tpu as pltpu
from jax.sharding import PartitionSpec as P

MESH = pl.DeviceIdType.MESH
F32, BF16 = jnp.float32, jnp.bfloat16
NT = (((1,), (1,)), ((), ()))
QROWS = 144


def wrap(v, n):
    return lax.rem(v + 4 * n, n)


def body(
    act_hbm, outg_hbm, in_hbm, out_hbm, ids_hbm, mask_hbm, queries, out, got,
    act, outg, proj_in, proj_out, ids, mask, q_pairs, q_wide, q_twin,
    part1, relay, mixed, recv1, sum1, recv2, act_low, grad_low, ids2, spread, perm, q_raw, q_perm, blocks, part, kept, theirs,
    vouch, in_sem, q_sem, id_sem, r_send, r_recv, s1_send, s1_recv, s2_send, s2_recv, s3_send, s3_recv, z1_send, z1_recv, z2_send, z2_recv,
    xy_send, xy_recv, o_send, o_recv, keep_sem,
):
    dp, tensor = lax.axis_index("dp"), lax.axis_index("tensor")
    x, zh, core = dp // 8, dp // 2 % 4, dp % 2
    zl, y = tensor // 4, tensor % 4
    twin = 1 - core
    z = zh * 4 + zl

    def device(dx=0, dy=0, dzh=0, dzl=0, c=core):
        return (
            (wrap(x + dx, 4) * 4 + wrap(zh + dzh, 4)) * 2 + c,
            wrap(zl + dzl, 4) * 4 + wrap(y + dy, 4),
        )

    def remote(src, dst, send, recv, dev):
        return pltpu.make_async_remote_copy(
            src_ref=src, dst_ref=dst, send_sem=send, recv_sem=recv, device_id=dev, device_id_type=MESH
        )

    loads = [
        pltpu.make_async_copy(src, dst, in_sem.at[k])
        for k, (src, dst) in enumerate([
            (in_hbm, proj_in), (act_hbm, act), (out_hbm, proj_out), (mask_hbm, mask), (outg_hbm, outg),
            (ids_hbm, ids), (queries, q_pairs),
        ])
    ]
    for load in loads:
        load.start()

    def along(d):
        to = lax.rem(z + 16 + d, 16)
        return ((x * 4 + to // 4) * 2 + core, lax.rem(to, 4) * 4 + y)

    barrier = pltpu.get_barrier_semaphore()
    peers = [along(1), along(-1), device(dx=1), device(dx=3), device(c=twin)]
    peers += [device(dy=d, c=c) for d in (1, 3) for c in (core, twin)]

    def vouch_for(n):
        pl.semaphore_signal(vouch.at[n, 0], inc=1, device_id=along(1), device_id_type=MESH)
        pl.semaphore_signal(vouch.at[n, 1], inc=1, device_id=along(-1), device_id_type=MESH)

    def hear(n):
        pl.semaphore_wait(vouch.at[n, 0], 1)
        pl.semaphore_wait(vouch.at[n, 1], 1)

    for peer in peers:
        pl.semaphore_signal(barrier, inc=1, device_id=peer, device_id_type=MESH)

    loads[0].wait()
    loads[1].wait()

    def relay_copy(half, layer):
        d = 3 if half else 1
        return remote(
            part1.at[wrap(y + 2, 4), layer, half], relay.at[half, layer], r_send.at[half, layer],
            r_recv.at[half, layer], device(dy=d),
        )

    def plain_copy(half, cross):
        d = 1 if half else 3
        c = twin if cross else core
        return remote(
            part1.at[wrap(y + d, 4), c, half], recv1.at[cross, 0, half], s1_send.at[cross, 0, half],
            s1_recv.at[cross, 0, half], device(dy=d, c=c),
        )

    def mixed_copy(half, cross):
        d = 3 if half else 1
        c = lax.rem(core + cross, 2)
        return remote(
            mixed.at[half, c], recv1.at[cross, 1, half], s1_send.at[cross, 1, half],
            s1_recv.at[cross, 1, half], device(dy=d, c=c),
        )

    def twin_copy(half):
        return remote(
            part1.at[y, twin, half], recv1.at[1, 2, half], s1_send.at[0, 2, half], s1_recv.at[0, 2, half],
            device(c=twin),
        )

    for layer in (0, 1):
        a = lax.dot_general(proj_in[layer], act[layer], NT, preferred_element_type=F32)
        for q in range(4):
            part1[q, layer, 0] = a[16 * q:16 * q + 16]
        if layer == 0:
            pl.semaphore_wait(barrier, len(peers))
            vouch_for(0)
        relay_copy(0, layer).start()
    for cross in (0, 1):
        plain_copy(0, cross).start()
    twin_copy(0).start()
    for load in loads[2:5]:
        load.wait()
    for layer in (0, 1):
        g = lax.dot_general(proj_out[layer], outg[layer], NT, preferred_element_type=F32) * mask[...].astype(F32)
        for q in range(4):
            for i in range(4):
                part1[q, layer, 1, :, 256 * i:256 * i + 256] = g[16 * i:16 * i + 16, 256 * q:256 * q + 256]
        relay_copy(1, layer).start()
    for cross in (0, 1):
        plain_copy(1, cross).start()
    twin_copy(1).start()
    loads[5].wait()
    ids2[core] = ids[...]
    id_copy = remote(ids, ids2.at[core], id_sem.at[0], id_sem.at[1], device(c=twin))
    id_copy.start()

    hear(0)
    vouch_for(1)

    loads[6].wait()

    def widen(step, carry):
        rows = pl.ds(pl.multiple_of(step * 512, 512), 512)
        q_wide[rows, :] = q_pairs[rows, :].astype(F32)
        return carry

    lax.fori_loop(0, 17, widen, 0)
    filler = jnp.zeros((QROWS - 136, 128), F32)

    def pick(layer, dst):
        def one(step, carry):
            rows = q_wide[pl.ds(2 * step + layer, 136, stride=64), :]
            dst[:, pl.ds(pl.multiple_of(step * 128, 128), 128)] = jnp.concatenate([rows, filler], axis=0).astype(BF16)
            return carry

        lax.fori_loop(0, 32, one, 0)

    pick(twin, q_twin)
    q_copy = remote(q_twin, q_raw.at[core], q_sem.at[0], q_sem.at[1], device(c=twin))
    q_copy.start()

    for half in (0, 1):
        for layer in (0, 1):
            relay_copy(half, layer).wait()
            mixed[half, layer] = relay[half, layer] + part1[wrap(y + (3 if half else 1), 4), layer, half]
            mixed_copy(half, jnp.where(core == layer, 0, 1)).start()

    hear(1)
    vouch_for(2)

    pick(core, q_raw.at[core])
    row = lax.broadcasted_iota(jnp.int32, (512, 1), 0)
    place = lax.rem(row // 16, 4) * 128 + row // 64 * 16 + lax.rem(row, 16)
    perm[...] = jnp.where(lax.broadcasted_iota(jnp.int32, (512, 512), 1) == place, 1.0, 0.0).astype(BF16)

    def second_copies(half):
        return [
            remote(
                sum1.at[half, wrap(zl + d, 4)], recv2.at[half, d - 1], s2_send.at[half, d - 1],
                s2_recv.at[half, d - 1], device(dzl=d),
            )
            for d in (2, 3, 1)
        ]

    for half in (0, 1):
        for cross in (0, 1):
            plain_copy(half, cross).wait()
            mixed_copy(half, cross).wait()
        twin_copy(half).wait()
        for cross in (0, 1):
            mine = recv1[1, 2, half] if cross else part1[y, core, half]
            total = mine + recv1[cross, 0, half] + recv1[cross, 1, half]
            for q in range(4):
                sum1[half, q, twin if cross else core] = total[:, 256 * q:256 * q + 256]
        for copy in second_copies(half):
            copy.start()

    q_copy.wait()

    def reorder(step, carry):
        b, half = step // 2, lax.rem(step, 2)
        columns = pl.ds(pl.multiple_of(step * 512, 512), 512)
        into = pl.ds(pl.multiple_of(half * 128, 128), 128)
        lhs = q_raw[:, :, columns].reshape(2 * QROWS, 512)
        moved = jnp.dot(lhs, perm[...], preferred_element_type=F32).astype(BF16).reshape(2, QROWS, 512)
        for q in range(4):
            q_perm[q * 4 + b, :, :, into] = moved[:, :, 128 * q:128 * q + 128]
        return carry

    lax.fori_loop(0, 4, reorder, 0)

    def third_copies(half):
        low, place = (grad_low, y) if half else (act_low, zl)
        return [
            remote(
                low.at[place], low.at[place], s3_send.at[half, d - 1], s3_recv.at[half, d - 1],
                device(dy=d) if half else device(dzl=d),
            )
            for d in (2, 1, 3)
        ]

    for half in (0, 1):
        for copy in second_copies(half):
            copy.wait()
        total = (sum1[half, zl] + recv2[half, 0] + recv2[half, 1] + recv2[half, 2]).astype(BF16)
        if half:
            grad_low[y] = total
        else:
            act_low[zl] = total
        for copy in third_copies(half):
            copy.start()

    lax.fori_loop(4, 8, reorder, 0)
    id_copy.wait()
    for half in (0, 1):
        for copy in third_copies(half):
            copy.wait_send()
    for d in (1, 2, 3):
        remote(
            act_low.at[wrap(zl - d, 4)], act_low.at[wrap(zl - d, 4)],
            s3_send.at[0, d - 1], s3_recv.at[0, d - 1], device(dzl=d),
        ).wait_recv()
        remote(
            grad_low.at[wrap(y - d, 4)], grad_low.at[wrap(y - d, 4)],
            s3_send.at[1, d - 1], s3_recv.at[1, d - 1], device(dy=d),
        ).wait_recv()

    lane = lax.broadcasted_iota(jnp.int32, (16, 256), 1)
    repeat = jnp.where(lane % 16 == lax.broadcasted_iota(jnp.int32, (16, 256), 0), 1.0, 0.0).astype(BF16)

    for row in (0, 1):
        sums = jnp.zeros((256, 16), F32)
        for q in range(4):
            onehot = lax.broadcasted_iota(jnp.int32, (16, 256), 0) == ids2[row, :, 256 * q:256 * q + 256]
            grads = grad_low[q, row].astype(F32)
            for i in range(16):
                spread[16 * i:16 * i + 16, :] = jnp.where(onehot, grads[i:i + 1], 0.0).astype(BF16)
            sums = sums + lax.dot_general(spread[...], act_low[q, row], NT, preferred_element_type=F32)
        wide = jnp.dot(sums.astype(BF16), repeat, preferred_element_type=F32)
        block = jnp.zeros((16, 256), F32)
        for i in range(16):
            block = block + jnp.where(lane // 16 == i, wide[16 * i:16 * i + 16], 0.0)
        blocks[row, 0, 0, 4] = block.astype(BF16)

    reach = (1, 2, 3, 4, -1, -2, -3, -4)
    z1 = {
        d: remote(
            blocks.at[:, 0, 0, 4], blocks.at[:, 0, 0, 4 - d], z1_send.at[k], z1_recv.at[k], along(d)
        )
        for k, d in enumerate(reach)
    }
    hear(2)
    for d in (-1, -2, -3, -4, 1, 2, 3, 4):
        z1[d].start()
    beyond = [
        remote(
            blocks.at[:, 0, 0, pl.ds(5, 4)], blocks.at[:, 0, 0, pl.ds(9, 4)], z2_send.at[0], z2_recv.at[0], along(-4)
        ),
        remote(
            blocks.at[:, 0, 0, pl.ds(1, 3)], blocks.at[:, 0, 0, pl.ds(13, 3)], z2_send.at[1], z2_recv.at[1], along(4)
        ),
    ]
    ways = [device(dx=1), device(dx=3), device(dy=1), device(dy=3)]
    groups = (((3, 2), (5, 1)), ((6, 1), (7, 2)), ((0, 2), (2, 1)), ((9, 2), (11, 2)), ((13, 1), (14, 2)))

    def stage(group, n):
        (start, one), (middle, two) = groups[group]
        whole, lower, upper = pl.ds(start, one + two), pl.ds(start, one), pl.ds(middle, two)
        at, both, rest = (lambda *k: blocks.at[k]), slice(None), pl.ds(1, 3)
        if n == 0:
            src = [at(both, 0, 0, whole)] * 4
            dst = [at(both, 0, 3, whole), at(both, 0, 1, whole), at(both, 3, 0, whole), at(both, 1, 0, whole)]
        elif n == 1:
            src = [at(0, 0, 3, whole), at(1, 0, 1, whole), at(0, 3, 0, whole), at(1, 1, 0, whole)]
            dst = [at(0, 0, 2, whole), at(1, 0, 2, whole), at(0, 2, 0, whole), at(1, 2, 0, whole)]
        elif n == 2:
            src = [at(1, rest, 0, whole)] * 2 + [at(0, 0, rest, whole)] * 2
            dst = [at(1, rest, 3, whole), at(1, rest, 1, whole), at(0, 3, rest, whole), at(0, 1, rest, whole)]
        else:
            src = [at(1, rest, 3, lower), at(1, rest, 1, upper), at(0, 3, rest, lower), at(0, 1, rest, upper)]
            dst = [at(1, rest, 2, lower), at(1, rest, 2, upper), at(0, 2, rest, lower), at(0, 2, rest, upper)]
        return [
            remote(src[k], dst[k], xy_send.at[group, n, k], xy_recv.at[group, n, k], ways[k]) for k in range(4)
        ]

    stages = {(group, n): stage(group, n) for group in range(5) for n in range(4)}

    def go(group, n):
        if n:
            before = stages[group, n - 1]
        else:
            before = ([z1[1], z1[-1]], [z1[-2], z1[-3], z1[-4]], [z1[2], z1[3], z1[4]], beyond[:1], beyond[1:])[group]
        for copy in before:
            copy.wait_recv()
        if n < 4:
            for copy in stages[group, n]:
                copy.start()

    def score(start, pairs, single, who=None):
        def add(place, places):
            far = lax.rem(z + place + 12, 16)
            zone, b = far // 4, lax.rem(far, 4)
            scores = jnp.zeros(((2 if who is None else 1) * QROWS, 128 * len(places)), F32)
            for dy in range(4):
                k = wrap(y + dy, 4) * 4 + b
                lhs = q_perm[k].reshape(2 * QROWS, 256) if who is None else q_perm[k, who]
                rhs = jnp.concatenate(
                    [blocks[half, dy, dx, place + e] for e in places for dx in range(4) for half in (0, 1)], axis=0
                )
                scores = scores + lax.dot_general(lhs, rhs, NT, preferred_element_type=F32)
            for k in range(len(places)):
                for n, rows in enumerate((0, 1) if who is None else (who,)):
                    part[rows, lax.rem(zone + k, 4)] += scores[QROWS * n:QROWS * n + QROWS, 128 * k:128 * k + 128]

        def add_pair(place, carry):
            add(place, (0, 4))
            return carry

        lax.fori_loop(start, start + pairs, add_pair, 0)
        add(single, (0,))

    part[...] = jnp.zeros_like(part)
    near, far = (0, 1, 2), (3, 4)
    for groups_now, n in [
        (near, 0), (near, 1), (far, 0), (far, 1), (near, 2), (far, 2), (near, 3), (far, 3), (near, 4), (far, 4)
    ]:
        for group in groups_now:
            go(group, n)
            if n == 0 and group in (1, 2):
                beyond[group - 1].start()
        if n == 4 and groups_now == near:
            score(0, 4, 8)

    def arrange(rows, into):
        for dx in range(4):
            cols = slice(32 * dx, 32 * dx + 32)
            pieces = [part[rows, zone][:136, cols] for zone in range(4)]
            into[:, pl.ds(pl.multiple_of(wrap(x + dx, 4) * 128, 128), 128)] = jnp.concatenate(pieces, axis=1)

    score(9, 3, 12, twin)
    arrange(twin, theirs)
    swap = remote(theirs, got, o_send.at[0], o_recv.at[0], device(c=twin))
    swap.start()
    score(9, 3, 12, core)
    arrange(core, kept)
    keep = pltpu.make_async_copy(kept, out, keep_sem)
    keep.start()

    for copy in z1.values():
        copy.wait_send()
    for copy in beyond:
        copy.wait_send()
    for copies in stages.values():
        for copy in copies:
            copy.wait_send()
    keep.wait()
    swap.wait()


def local(activations, out_grads, proj_in, proj_out, example_ids, loss_mask, query_grads):
    queries = query_grads.reshape(136, 2, 32, 128).transpose(0, 2, 1, 3).reshape(136 * 64, 128)
    dma = pltpu.SemaphoreType.DMA
    own, received = pl.pallas_call(
        body,
        out_shape=[jax.ShapeDtypeStruct((136, 512), F32)] * 2,
        in_specs=[pl.BlockSpec(memory_space=pl.ANY)] * 7,
        out_specs=[pl.BlockSpec(memory_space=pl.ANY)] * 2,
        scratch_shapes=[
            pltpu.VMEM((2, 1024, 256), BF16),
            pltpu.VMEM((2, 1024, 256), BF16),
            pltpu.VMEM((2, 64, 256), BF16),
            pltpu.VMEM((2, 64, 256), BF16),
            pltpu.VMEM((1, 1024), jnp.int32),
            pltpu.VMEM((1, 1024), jnp.int32),
            pltpu.VMEM((136 * 64, 128), BF16),
            pltpu.VMEM((136 * 64, 128), F32),
            pltpu.VMEM((QROWS, 4096), BF16),
            pltpu.VMEM((4, 2, 2, 16, 1024), F32),
            pltpu.VMEM((2, 2, 16, 1024), F32),
            pltpu.VMEM((2, 2, 16, 1024), F32),
            pltpu.VMEM((2, 3, 2, 16, 1024), F32),
            pltpu.VMEM((2, 4, 2, 16, 256), F32),
            pltpu.VMEM((2, 3, 2, 16, 256), F32),
            pltpu.VMEM((4, 2, 16, 256), BF16),
            pltpu.VMEM((4, 2, 16, 256), BF16),
            pltpu.VMEM((2, 1, 1024), jnp.int32),
            pltpu.VMEM((256, 256), BF16),
            pltpu.VMEM((512, 512), BF16),
            pltpu.VMEM((2, QROWS, 4096), BF16),
            pltpu.VMEM((16, 2, QROWS, 256), BF16),
            pltpu.VMEM((2, 4, 4, 16, 16, 256), BF16),
            pltpu.VMEM((2, 4, QROWS, 128), F32),
            pltpu.VMEM((136, 512), F32),
            pltpu.VMEM((136, 512), F32),
            pltpu.SemaphoreType.REGULAR((3, 2)), dma((7,)), dma((2,)), dma((2,)), dma((2, 2)), dma((2, 2)), dma((2, 3, 2)), dma((2, 3, 2)),
            dma((2, 3)), dma((2, 3)), dma((2, 3)), dma((2, 3)), dma((8,)), dma((8,)), dma((2,)), dma((2,)),
            dma((5, 4, 4)), dma((5, 4, 4)), dma((1,)), dma((1,)), dma,
        ],
        compiler_params=pltpu.CompilerParams(
            collective_id=0, has_side_effects=True, vmem_limit_bytes=56 * 2**20
        ),
        name="scores",
    )(activations, out_grads, proj_in, proj_out, example_ids, loss_mask, queries)
    return own + received


def solution(mesh):
    in_specs = (
        P(None, "dp", "tensor"),
        P(None, "dp", "tensor"),
        P(None, None, "tensor"),
        P(None, None, "tensor"),
        P("dp", None),
        P("dp", None),
        P(("dp", "tensor"), None, None),
    )
    out_specs = P(("dp", "tensor"), None)
    return jax.shard_map(local, mesh=mesh, in_specs=in_specs, out_specs=out_specs, check_vma=False)
```

```python
import jax
import jax.numpy as jnp
from jax import lax
from jax.experimental import pallas as pl
from jax.experimental.pallas import tpu as pltpu
from jax.sharding import PartitionSpec as P

MESH = pl.DeviceIdType.MESH
F32, BF16 = jnp.float32, jnp.bfloat16
NT = (((1,), (1,)), ((), ()))
QROWS = 144


def wrap(v, n):
    return lax.rem(v + 4 * n, n)


def body(
    act_hbm, outg_hbm, in_hbm, out_hbm, ids_hbm, mask_hbm, queries, out, got,
    act, outg, proj_in, proj_out, ids, mask, q_pairs, q_wide, q_twin,
    part1, relay, mixed, recv1, sum1, recv2, act_low, grad_low, ids2, spread, perm, q_raw, q_perm, blocks, part, kept, theirs,
    vouch, in_sem, q_sem, id_sem, r_send, r_recv, s1_send, s1_recv, s2_send, s2_recv, s3_send, s3_recv, z1_send, z1_recv, z2_send, z2_recv,
    xy_send, xy_recv, o_send, o_recv, keep_sem,
):
    dp, tensor = lax.axis_index("dp"), lax.axis_index("tensor")
    x, zh, core = dp // 8, dp // 2 % 4, dp % 2
    zl, y = tensor // 4, tensor % 4
    twin = 1 - core
    z = zh * 4 + zl

    def device(dx=0, dy=0, dzh=0, dzl=0, c=core):
        return (
            (wrap(x + dx, 4) * 4 + wrap(zh + dzh, 4)) * 2 + c,
            wrap(zl + dzl, 4) * 4 + wrap(y + dy, 4),
        )

    def remote(src, dst, send, recv, dev):
        return pltpu.make_async_remote_copy(
            src_ref=src, dst_ref=dst, send_sem=send, recv_sem=recv, device_id=dev, device_id_type=MESH
        )

    loads = [
        pltpu.make_async_copy(src, dst, in_sem.at[k])
        for k, (src, dst) in enumerate([
            (in_hbm, proj_in), (act_hbm, act), (out_hbm, proj_out), (mask_hbm, mask), (outg_hbm, outg),
            (ids_hbm, ids), (queries, q_pairs),
        ])
    ]
    for load in loads:
        load.start()

    def along(d):
        to = lax.rem(z + 16 + d, 16)
        return ((x * 4 + to // 4) * 2 + core, lax.rem(to, 4) * 4 + y)

    barrier = pltpu.get_barrier_semaphore()
    peers = [along(1), along(-1), device(dx=1), device(dx=3), device(c=twin)]
    peers += [device(dy=d, c=c) for d in (1, 3) for c in (core, twin)]

    def vouch_for(n):
        pl.semaphore_signal(vouch.at[n, 0], inc=1, device_id=along(1), device_id_type=MESH)
        pl.semaphore_signal(vouch.at[n, 1], inc=1, device_id=along(-1), device_id_type=MESH)

    def hear(n):
        pl.semaphore_wait(vouch.at[n, 0], 1)
        pl.semaphore_wait(vouch.at[n, 1], 1)

    for peer in peers:
        pl.semaphore_signal(barrier, inc=1, device_id=peer, device_id_type=MESH)

    loads[0].wait()
    loads[1].wait()

    def relay_copy(half, layer):
        d = 3 if half else 1
        return remote(
            part1.at[wrap(y + 2, 4), layer, half], relay.at[half, layer], r_send.at[half, layer],
            r_recv.at[half, layer], device(dy=d),
        )

    def plain_copy(half, cross):
        d = 1 if half else 3
        c = twin if cross else core
        return remote(
            part1.at[wrap(y + d, 4), c, half], recv1.at[cross, 0, half], s1_send.at[cross, 0, half],
            s1_recv.at[cross, 0, half], device(dy=d, c=c),
        )

    def mixed_copy(half, cross):
        d = 3 if half else 1
        c = lax.rem(core + cross, 2)
        return remote(
            mixed.at[half, c], recv1.at[cross, 1, half], s1_send.at[cross, 1, half],
            s1_recv.at[cross, 1, half], device(dy=d, c=c),
        )

    def twin_copy(half):
        return remote(
            part1.at[y, twin, half], recv1.at[1, 2, half], s1_send.at[0, 2, half], s1_recv.at[0, 2, half],
            device(c=twin),
        )

    for layer in (0, 1):
        a = lax.dot_general(proj_in[layer], act[layer], NT, preferred_element_type=F32)
        for q in range(4):
            part1[q, layer, 0] = a[16 * q:16 * q + 16]
        if layer == 0:
            pl.semaphore_wait(barrier, len(peers))
            vouch_for(0)
        relay_copy(0, layer).start()
    for cross in (0, 1):
        plain_copy(0, cross).start()
    twin_copy(0).start()
    for load in loads[2:5]:
        load.wait()
    for layer in (0, 1):
        g = lax.dot_general(proj_out[layer], outg[layer], NT, preferred_element_type=F32) * mask[...].astype(F32)
        for q in range(4):
            for i in range(4):
                part1[q, layer, 1, :, 256 * i:256 * i + 256] = g[16 * i:16 * i + 16, 256 * q:256 * q + 256]
        relay_copy(1, layer).start()
    for cross in (0, 1):
        plain_copy(1, cross).start()
    twin_copy(1).start()
    loads[5].wait()
    ids2[core] = ids[...]
    id_copy = remote(ids, ids2.at[core], id_sem.at[0], id_sem.at[1], device(c=twin))
    id_copy.start()

    hear(0)
    vouch_for(1)

    loads[6].wait()

    def widen(step, carry):
        rows = pl.ds(pl.multiple_of(step * 512, 512), 512)
        q_wide[rows, :] = q_pairs[rows, :].astype(F32)
        return carry

    lax.fori_loop(0, 17, widen, 0)
    filler = jnp.zeros((QROWS - 136, 128), F32)

    def pick(layer, dst):
        def one(step, carry):
            rows = q_wide[pl.ds(2 * step + layer, 136, stride=64), :]
            dst[:, pl.ds(pl.multiple_of(step * 128, 128), 128)] = jnp.concatenate([rows, filler], axis=0).astype(BF16)
            return carry

        lax.fori_loop(0, 32, one, 0)

    pick(twin, q_twin)
    q_copy = remote(q_twin, q_raw.at[core], q_sem.at[0], q_sem.at[1], device(c=twin))
    q_copy.start()

    for half in (0, 1):
        for layer in (0, 1):
            relay_copy(half, layer).wait()
            mixed[half, layer] = relay[half, layer] + part1[wrap(y + (3 if half else 1), 4), layer, half]
            mixed_copy(half, jnp.where(core == layer, 0, 1)).start()

    hear(1)
    vouch_for(2)

    pick(core, q_raw.at[core])
    row = lax.broadcasted_iota(jnp.int32, (512, 1), 0)
    place = lax.rem(row // 16, 4) * 128 + row // 64 * 16 + lax.rem(row, 16)
    perm[...] = jnp.where(lax.broadcasted_iota(jnp.int32, (512, 512), 1) == place, 1.0, 0.0).astype(BF16)

    def second_copies(half):
        return [
            remote(
                sum1.at[half, wrap(zl + d, 4)], recv2.at[half, d - 1], s2_send.at[half, d - 1],
                s2_recv.at[half, d - 1], device(dzl=d),
            )
            for d in (2, 3, 1)
        ]

    for half in (0, 1):
        for cross in (0, 1):
            plain_copy(half, cross).wait()
            mixed_copy(half, cross).wait()
        twin_copy(half).wait()
        for cross in (0, 1):
            mine = recv1[1, 2, half] if cross else part1[y, core, half]
            total = mine + recv1[cross, 0, half] + recv1[cross, 1, half]
            for q in range(4):
                sum1[half, q, twin if cross else core] = total[:, 256 * q:256 * q + 256]
        for copy in second_copies(half):
            copy.start()

    q_copy.wait()

    def reorder(step, carry):
        b, half = step // 2, lax.rem(step, 2)
        columns = pl.ds(pl.multiple_of(step * 512, 512), 512)
        into = pl.ds(pl.multiple_of(half * 128, 128), 128)
        lhs = q_raw[:, :, columns].reshape(2 * QROWS, 512)
        moved = jnp.dot(lhs, perm[...], preferred_element_type=F32).astype(BF16).reshape(2, QROWS, 512)
        for q in range(4):
            q_perm[q * 4 + b, :, :, into] = moved[:, :, 128 * q:128 * q + 128]
        return carry

    lax.fori_loop(0, 4, reorder, 0)

    def third_copies(half):
        low, place = (grad_low, y) if half else (act_low, zl)
        return [
            remote(
                low.at[place], low.at[place], s3_send.at[half, d - 1], s3_recv.at[half, d - 1],
                device(dy=d) if half else device(dzl=d),
            )
            for d in (2, 1, 3)
        ]

    for half in (0, 1):
        for copy in second_copies(half):
            copy.wait()
        total = (sum1[half, zl] + recv2[half, 0] + recv2[half, 1] + recv2[half, 2]).astype(BF16)
        if half:
            grad_low[y] = total
        else:
            act_low[zl] = total
        for copy in third_copies(half):
            copy.start()

    lax.fori_loop(4, 8, reorder, 0)
    id_copy.wait()
    for half in (0, 1):
        for copy in third_copies(half):
            copy.wait_send()
    for d in (1, 2, 3):
        remote(
            act_low.at[wrap(zl - d, 4)], act_low.at[wrap(zl - d, 4)],
            s3_send.at[0, d - 1], s3_recv.at[0, d - 1], device(dzl=d),
        ).wait_recv()
        remote(
            grad_low.at[wrap(y - d, 4)], grad_low.at[wrap(y - d, 4)],
            s3_send.at[1, d - 1], s3_recv.at[1, d - 1], device(dy=d),
        ).wait_recv()

    lane = lax.broadcasted_iota(jnp.int32, (16, 256), 1)
    repeat = jnp.where(lane % 16 == lax.broadcasted_iota(jnp.int32, (16, 256), 0), 1.0, 0.0).astype(BF16)

    for row in (0, 1):
        sums = jnp.zeros((256, 16), F32)
        for q in range(4):
            onehot = lax.broadcasted_iota(jnp.int32, (16, 256), 0) == ids2[row, :, 256 * q:256 * q + 256]
            grads = grad_low[q, row].astype(F32)
            for i in range(16):
                spread[16 * i:16 * i + 16, :] = jnp.where(onehot, grads[i:i + 1], 0.0).astype(BF16)
            sums = sums + lax.dot_general(spread[...], act_low[q, row], NT, preferred_element_type=F32)
        wide = jnp.dot(sums.astype(BF16), repeat, preferred_element_type=F32)
        block = jnp.zeros((16, 256), F32)
        for i in range(16):
            block = block + jnp.where(lane // 16 == i, wide[16 * i:16 * i + 16], 0.0)
        blocks[row, 0, 0, 4] = block.astype(BF16)

    reach = (1, 2, 3, 4, -1, -2, -3, -4)
    z1 = {
        d: remote(
            blocks.at[:, 0, 0, 4], blocks.at[:, 0, 0, 4 - d], z1_send.at[k], z1_recv.at[k], along(d)
        )
        for k, d in enumerate(reach)
    }
    hear(2)
    for d in (-1, -2, -3, -4, 1, 2, 3, 4):
        z1[d].start()
    beyond = [
        remote(
            blocks.at[:, 0, 0, pl.ds(5, 4)], blocks.at[:, 0, 0, pl.ds(9, 4)], z2_send.at[0], z2_recv.at[0], along(-4)
        ),
        remote(
            blocks.at[:, 0, 0, pl.ds(1, 3)], blocks.at[:, 0, 0, pl.ds(13, 3)], z2_send.at[1], z2_recv.at[1], along(4)
        ),
    ]
    ways = [device(dx=1), device(dx=3), device(dy=1), device(dy=3)]
    groups = (((3, 2), (5, 1)), ((6, 1), (7, 2)), ((0, 2), (2, 1)), ((9, 2), (11, 2)), ((13, 1), (14, 2)))

    def stage(group, n):
        (start, one), (middle, two) = groups[group]
        whole, lower, upper = pl.ds(start, one + two), pl.ds(start, one), pl.ds(middle, two)
        at, both, rest = (lambda *k: blocks.at[k]), slice(None), pl.ds(1, 3)
        if n == 0:
            src = [at(both, 0, 0, whole)] * 4
            dst = [at(both, 0, 3, whole), at(both, 0, 1, whole), at(both, 3, 0, whole), at(both, 1, 0, whole)]
        elif n == 1:
            src = [at(0, 0, 3, whole), at(1, 0, 1, whole), at(0, 3, 0, whole), at(1, 1, 0, whole)]
            dst = [at(0, 0, 2, whole), at(1, 0, 2, whole), at(0, 2, 0, whole), at(1, 2, 0, whole)]
        elif n == 2:
            src = [at(1, rest, 0, whole)] * 2 + [at(0, 0, rest, whole)] * 2
            dst = [at(1, rest, 3, whole), at(1, rest, 1, whole), at(0, 3, rest, whole), at(0, 1, rest, whole)]
        else:
            src = [at(1, rest, 3, lower), at(1, rest, 1, upper), at(0, 3, rest, lower), at(0, 1, rest, upper)]
            dst = [at(1, rest, 2, lower), at(1, rest, 2, upper), at(0, 2, rest, lower), at(0, 2, rest, upper)]
        return [
            remote(src[k], dst[k], xy_send.at[group, n, k], xy_recv.at[group, n, k], ways[k]) for k in range(4)
        ]

    stages = {(group, n): stage(group, n) for group in range(5) for n in range(4)}

    def go(group, n):
        if n:
            before = stages[group, n - 1]
        else:
            before = ([z1[1], z1[-1]], [z1[-2], z1[-3], z1[-4]], [z1[2], z1[3], z1[4]], beyond[:1], beyond[1:])[group]
        for copy in before:
            copy.wait_recv()
        if n < 4:
            for copy in stages[group, n]:
                copy.start()

    def score(start, pairs, single, who=None):
        def add(place, places):
            far = lax.rem(z + place + 12, 16)
            zone, b = far // 4, lax.rem(far, 4)
            scores = jnp.zeros(((2 if who is None else 1) * QROWS, 128 * len(places)), F32)
            for dy in range(4):
                k = wrap(y + dy, 4) * 4 + b
                lhs = q_perm[k].reshape(2 * QROWS, 256) if who is None else q_perm[k, who]
                rhs = jnp.concatenate(
                    [blocks[half, dy, dx, place + e] for e in places for dx in range(4) for half in (0, 1)], axis=0
                )
                scores = scores + lax.dot_general(lhs, rhs, NT, preferred_element_type=F32)
            for k in range(len(places)):
                for n, rows in enumerate((0, 1) if who is None else (who,)):
                    part[rows, lax.rem(zone + k, 4)] += scores[QROWS * n:QROWS * n + QROWS, 128 * k:128 * k + 128]

        def add_pair(place, carry):
            add(place, (0, 4))
            return carry

        lax.fori_loop(start, start + pairs, add_pair, 0)
        add(single, (0,))

    part[...] = jnp.zeros_like(part)
    near, far = (0, 1, 2), (3, 4)
    for groups_now, n in [
        (near, 0), (near, 1), (far, 0), (far, 1), (near, 2), (far, 2), (near, 3), (far, 3), (near, 4), (far, 4)
    ]:
        for group in groups_now:
            go(group, n)
            if n == 0 and group in (1, 2):
                beyond[group - 1].start()
        if n == 4 and groups_now == near:
            score(0, 4, 8)

    def arrange(rows, into):
        for dx in range(4):
            cols = slice(32 * dx, 32 * dx + 32)
            pieces = [part[rows, zone][:136, cols] for zone in range(4)]
            into[:, pl.ds(pl.multiple_of(wrap(x + dx, 4) * 128, 128), 128)] = jnp.concatenate(pieces, axis=1)

    score(9, 3, 12, twin)
    arrange(twin, theirs)
    swap = remote(theirs, got, o_send.at[0], o_recv.at[0], device(c=twin))
    swap.start()
    score(9, 3, 12, core)
    arrange(core, kept)
    keep = pltpu.make_async_copy(kept, out, keep_sem)
    keep.start()

    for copy in z1.values():
        copy.wait_send()
    for copy in beyond:
        copy.wait_send()
    for copies in stages.values():
        for copy in copies:
            copy.wait_send()
    keep.wait()
    swap.wait()


def local(activations, out_grads, proj_in, proj_out, example_ids, loss_mask, query_grads):
    queries = query_grads.reshape(136, 2, 32, 128).transpose(0, 2, 1, 3).reshape(136 * 64, 128)
    dma = pltpu.SemaphoreType.DMA
    own, received = pl.pallas_call(
        body,
        out_shape=[jax.ShapeDtypeStruct((136, 512), F32)] * 2,
        in_specs=[pl.BlockSpec(memory_space=pl.ANY)] * 7,
        out_specs=[pl.BlockSpec(memory_space=pl.ANY)] * 2,
        scratch_shapes=[
            pltpu.VMEM((2, 1024, 256), BF16),
            pltpu.VMEM((2, 1024, 256), BF16),
            pltpu.VMEM((2, 64, 256), BF16),
            pltpu.VMEM((2, 64, 256), BF16),
            pltpu.VMEM((1, 1024), jnp.int32),
            pltpu.VMEM((1, 1024), jnp.int32),
            pltpu.VMEM((136 * 64, 128), BF16),
            pltpu.VMEM((137 * 64, 128), F32),
            pltpu.VMEM((QROWS, 4096), BF16),
            pltpu.VMEM((4, 2, 2, 16, 1024), F32),
            pltpu.VMEM((2, 2, 16, 1024), F32),
            pltpu.VMEM((2, 2, 16, 1024), F32),
            pltpu.VMEM((2, 3, 2, 16, 1024), F32),
            pltpu.VMEM((2, 4, 2, 16, 256), F32),
            pltpu.VMEM((2, 3, 2, 16, 256), F32),
            pltpu.VMEM((4, 2, 16, 256), BF16),
            pltpu.VMEM((4, 2, 16, 256), BF16),
            pltpu.VMEM((2, 1, 1024), jnp.int32),
            pltpu.VMEM((256, 256), BF16),
            pltpu.VMEM((512, 512), BF16),
            pltpu.VMEM((2, QROWS, 4096), BF16),
            pltpu.VMEM((16, 2, QROWS, 256), BF16),
            pltpu.VMEM((2, 4, 4, 16, 16, 256), BF16),
            pltpu.VMEM((2, 4, QROWS, 128), F32),
            pltpu.VMEM((136, 512), F32),
            pltpu.VMEM((136, 512), F32),
            pltpu.SemaphoreType.REGULAR((3, 2)), dma((7,)), dma((2,)), dma((2,)), dma((2, 2)), dma((2, 2)), dma((2, 3, 2)), dma((2, 3, 2)),
            dma((2, 3)), dma((2, 3)), dma((2, 3)), dma((2, 3)), dma((8,)), dma((8,)), dma((2,)), dma((2,)),
            dma((5, 4, 4)), dma((5, 4, 4)), dma((1,)), dma((1,)), dma,
        ],
        compiler_params=pltpu.CompilerParams(
            collective_id=0, has_side_effects=True, vmem_limit_bytes=56 * 2**20
        ),
        name="scores",
    )(activations, out_grads, proj_in, proj_out, example_ids, loss_mask, queries)
    return own + received


def solution(mesh):
    in_specs = (
        P(None, "dp", "tensor"),
        P(None, "dp", "tensor"),
        P(None, None, "tensor"),
        P(None, None, "tensor"),
        P("dp", None),
        P("dp", None),
        P(("dp", "tensor"), None, None),
    )
    out_specs = P(("dp", "tensor"), None)
    return jax.shard_map(local, mesh=mesh, in_specs=in_specs, out_specs=out_specs, check_vma=False)
```
